32 devices in a mesh: pipe: 4 (over x, core), ctx: 2 (over y), tp: 4 (over z).
Axes of the slice: x: 2, y: 2, z: 4, core: 2. Of those that a mesh axis runs over, the one named last changes fastest.
Arguments:
- query_rows: bfloat16 [1024, 64, 128], P(('pipe', 'ctx'), 'tp'), may hold values from -100 to 100
- key_rows: bfloat16 [1024, 4, 128], P(('pipe', 'ctx'), 'tp'), may hold values from -6 to 6
- value_rows: bfloat16 [1024, 4, 128], P(('pipe', 'ctx'), 'tp'), may hold values from -6 to 6
- doc_ids: int32 [1024], P(('pipe', 'ctx')), may hold values from 0 to 3, never falling along the last dimension, each value on 1 to 512 neighbouring positions
- out_weight: bfloat16 [8192, 8192], P('tp', 'ctx'), may hold values from -0.25 to 0.25
Outputs:
- projected: bfloat16 [4, 2, 4, 32, 8192], P('pipe', None, 'tp', None, 'ctx')
The draws below stay inside these ranges and needn't reach their ends.
Inputs may be any that keep to these rules, and one draw needn't show every extreme that they name: `doc_ids`: ids never fall along the book; the longest document has exactly 512 tokens.
All inputs are finite; a program needn't handle non-finite values.
Results may differ from the reference program's by a relative error of at most 0.012.
Values may be sent and summed in bfloat16 or wider, within the bound.
No kernel may reach another device: no remote copies, remote signals or barrier semaphores. Data moves between devices by JAX's collectives and lax.ppermute only.
A program may use at most 128 MiB of HBM per device.

```python
import math
import jax
import jax.numpy as jnp
import numpy as np
from jax import lax

HD = 128
QH = 64
KVH = 4
DW = 8192
TOK_DEV = 128
DOCS = 4
TOKENS = 1024
N_PIPE = 4
N_CTX = 2
N_TP = 4


def shared_keys(key):
    base_keys = jax.random.normal(jax.random.fold_in(key, 11), (TOKENS, KVH, HD), jnp.float32) * 1.3
    base_keys = jnp.clip(base_keys, -5.5, 5.5)
    return base_keys


def draw_key_rows(key, part):
    return shared_keys(key).astype(jnp.bfloat16)


def draw_query_rows(key, part):
    drawn_query = jax.random.normal(jax.random.fold_in(key, 12), (TOKENS, QH, HD), jnp.float32) * 1.5
    drawn_query = jnp.clip(drawn_query, -9.0, 9.0)
    return drawn_query.astype(jnp.bfloat16)


def level_of(stream_key, shape, split, low, largest):
    def one(axis_at, shards_of):
        heights = jax.random.uniform(jax.random.fold_in(jax.random.fold_in(stream_key, 6), axis_at), (shards_of,), jnp.float32, low / len(split), largest / len(split))
        return jnp.repeat(jnp.exp(heights), shape[axis_at] // shards_of).reshape((-1,) + (1,) * (len(shape) - axis_at - 1))

    level = one(*split[0])
    for cut in split[1:]:
        level = level * one(*cut)
    return level


def split_up(number_of, total, limit, lean):
    portions = [(1 << 20) // math.isqrt(rank ** lean) + 1 for rank in range(2, number_of + 1)]
    rest, given = total - limit - (number_of - 1), [1] * (number_of - 1)
    while rest > 0:
        movable = [i for i in range(number_of - 1) if given[i] < limit]
        mass, budget = sum([portions[i] for i in movable]), rest
        for i in movable:
            addition = min(limit - given[i], max(1, budget * portions[i] // mass), rest)
            given[i] = given[i] + addition
            rest = rest - addition
    return np.array([limit] + given)


def ragged_sizes(own_key, number_of, total, reach, slope):
    if number_of == 2:
        one = jax.random.randint(own_key, (), max(1, total - reach), min(reach, total - 1) + 1)
        return jnp.stack([one, total - one])
    tallies = jnp.asarray(split_up(number_of, total, reach, slope), jnp.int32)
    pairs = (number_of - 1) // 2
    donor, sink = tallies[1:1 + 2 * pairs:2], tallies[2:2 + 2 * pairs:2]
    margin = jnp.minimum(donor - 1, reach - sink)
    passed = jax.random.randint(jax.random.fold_in(own_key, 1), (pairs,), 0, 1 << 20) % (margin + 1)
    tallies = tallies.at[1:1 + 2 * pairs:2].set(donor - passed).at[2:2 + 2 * pairs:2].set(sink + passed)
    return tallies[jax.random.permutation(jax.random.fold_in(own_key, 2), number_of)]


def scatter_about(rng, extent, width, most, shards=(), kind=jnp.bfloat16):
    gain = level_of(rng, extent, shards, -0.22, 0.18) if shards else 1.0
    array = jax.random.normal(rng, extent, jnp.float32) * width * gain
    return jnp.minimum(jnp.maximum(array, -most), most).astype(kind)


def setup_inputs(seed: int = 0) -> dict:
    key_list = jax.random.split(jax.random.key(seed), 6)
    return {
        "query_rows": draw_query_rows(jax.random.fold_in(key_list[5], 71), 0),
        "key_rows": draw_key_rows(jax.random.fold_in(key_list[5], 71), 0),
        "value_rows": scatter_about(key_list[2], (TOKENS, KVH, HD), 1.0, 6.0, ((0, 8), (1, 4))),
        "doc_ids": jnp.searchsorted(jnp.cumsum(ragged_sizes(key_list[3], DOCS, TOKENS, TOKENS // 2, 0)), jnp.arange(TOKENS), side="right").astype(jnp.int32),
        "out_weight": scatter_about(key_list[4], (QH * HD, DW), (QH * HD // 16) ** -0.5, 0.25, ((0, 4), (1, 2))),
    }


def reference(query_rows, key_rows, value_rows, doc_ids, out_weight):
    group_size = QH // KVH
    inv_scale = HD ** -0.5
    block_rows = math.gcd(TOKENS, 512)
    pieces = []
    for row_begin in range(0, TOKENS, block_rows):
        row_end = row_begin + block_rows
        query_pos = jnp.arange(row_begin, row_end, dtype=jnp.int32)
        key_pos = jnp.arange(row_end, dtype=jnp.int32)
        allowed = (key_pos[None, :] <= query_pos[:, None]) & (doc_ids[None, :row_end] == doc_ids[row_begin:row_end][:, None])
        query_block = query_rows[row_begin:row_end].reshape(block_rows, KVH, group_size, HD).astype(jnp.float32)
        key_block = key_rows[:row_end].astype(jnp.float32)
        value_block = value_rows[:row_end].astype(jnp.float32)

        def per_head(head_index):
            query_head = lax.dynamic_index_in_dim(query_block, head_index, 1, keepdims=False)
            key_head = lax.dynamic_index_in_dim(key_block, head_index, 1, keepdims=False)
            value_head = lax.dynamic_index_in_dim(value_block, head_index, 1, keepdims=False)
            scores = jnp.einsum("bgd,kd->gbk", query_head, key_head) * inv_scale
            masked = jnp.where(allowed[None], scores, -1e30)
            row_peak = jnp.max(masked, axis=2, keepdims=True)
            weights = jnp.where(allowed[None], jnp.exp(scores - row_peak), 0.0)
            row_total = jnp.sum(weights, axis=2)
            rounded = lax.optimization_barrier(weights.astype(jnp.bfloat16)).astype(jnp.float32)
            combined = jnp.einsum("gbk,kd->bgd", rounded, value_head)
            return combined / jnp.transpose(row_total)[:, :, None]

        per_heads = lax.map(per_head, jnp.arange(KVH, dtype=jnp.int32))
        pieces.append(jnp.transpose(per_heads, (1, 0, 2, 3)).reshape(block_rows, QH * HD).astype(jnp.bfloat16))
    attention = jnp.concatenate(pieces, axis=0)
    projected = jnp.dot(attention, out_weight, preferred_element_type=jnp.float32).astype(jnp.bfloat16)
    return projected.reshape(N_PIPE, N_CTX, N_TP, TOK_DEV // N_TP, DW)
```

```python
import functools

import jax
import jax.numpy as jnp
from jax import lax
from jax.experimental import pallas as pl
from jax.experimental.pallas import tpu as pltpu
from jax.sharding import PartitionSpec as P

BF16 = jnp.bfloat16
F32 = jnp.float32
LOG2E = 1.4426950408889634
MIB = 1 << 20

ORDER = ((3, 2, 1, 0), (3, 2, 0, 1), (0, 1, 3, 2), (0, 1, 2, 3))
PLACE = tuple(tuple(row.index(s) for s in range(4)) for row in ORDER)
OUTER = ((0, 1), (1, 0), (2, 3), (3, 2))
INNER = ((1, 2), (2, 1))


def pack_kernel(key_ref, value_ref, doc_ref, out_ref):
    rows = key_ref.shape[0]
    out_ref[:rows] = key_ref[...]
    out_ref[rows : 2 * rows] = value_ref[...]
    marks = doc_ref[...].astype(F32)
    out_ref[2 * rows :] = jnp.broadcast_to(marks, (16, rows)).astype(BF16)


def pack(key_rows, value_rows, doc_ids):
    rows, _, width = key_rows.shape
    return pl.pallas_call(
        pack_kernel,
        out_shape=jax.ShapeDtypeStruct((2 * rows + 16, width), BF16),
        compiler_params=pltpu.CompilerParams(vmem_limit_bytes=4 * MIB),
    )(key_rows.reshape(rows, width), value_rows.reshape(rows, width), doc_ids.reshape(1, rows))


def attend_kernel(window, heads, info_ref, query_ref, *refs):
    blocks = refs[:8]
    out_ref, wide, keys, values, marks, bias = refs[8:]
    rows, width = blocks[0].shape[0] // 2 - 8, blocks[0].shape[1]
    mine, asked = info_ref[0], info_ref[1]
    keys[...] = jnp.zeros_like(keys)
    values[...] = jnp.zeros_like(values)
    marks[...] = jnp.full_like(marks, -1.0)
    for m in range(8):
        slot = (mine ^ m) - asked + window - 1

        @pl.when((slot >= 0) & (slot < window))
        def _(m=m, slot=slot):
            at = pl.ds(pl.multiple_of(slot * rows, rows), rows)
            keys[at, :] = blocks[m][:rows]
            values[at, :] = blocks[m][rows : 2 * rows]
            marks[slot] = blocks[m][2 * rows :].astype(F32)[:8]

    wide[...] = query_ref[...].astype(F32)
    own = jnp.transpose(jnp.broadcast_to(marks[window - 1][:1], (rows, rows)))
    for s in range(window):
        allowed = own == marks[s][:1]
        if s == window - 1:
            at_row = lax.broadcasted_iota(jnp.int32, (rows, rows), 0)
            at_col = lax.broadcasted_iota(jnp.int32, (rows, rows), 1)
            allowed = allowed & (at_col <= at_row)
        bias[:, s * rows : (s + 1) * rows] = jnp.where(allowed, 0.0, -1e30)
    factor = LOG2E * width**-0.5
    quarter = rows // 4
    for h in range(heads):
        query = wide[pl.ds(h, rows, stride=heads), :].astype(BF16)
        scores = lax.dot_general(
            query, keys[...], (((1,), (1,)), ((), ())), preferred_element_type=F32
        )
        scores = scores + bias[...]
        peak = jnp.max(scores, axis=1, keepdims=True)
        weights = jnp.exp2((scores - peak) * factor)
        total = jnp.sum(weights, axis=1, keepdims=True)
        summed = jnp.dot(weights.astype(BF16), values[...], preferred_element_type=F32)
        result = (summed / total).astype(BF16)
        for s in range(4):
            at = pl.ds(pl.multiple_of(info_ref[2 + s] * quarter, quarter), quarter)
            out_ref[at, h * width : (h + 1) * width] = result[s * quarter : (s + 1) * quarter]


def attend(info, query, blocks, window):
    rows, heads, width = query.shape
    vmem = pl.BlockSpec(memory_space=pltpu.VMEM)
    smem = pl.BlockSpec(memory_space=pltpu.SMEM)
    return pl.pallas_call(
        functools.partial(attend_kernel, window, heads),
        out_shape=jax.ShapeDtypeStruct((rows, heads * width), BF16),
        in_specs=[smem] + [vmem] * 9,
        out_specs=vmem,
        scratch_shapes=[
            pltpu.VMEM((rows * heads, width), F32),
            pltpu.VMEM((window * rows, width), BF16),
            pltpu.VMEM((window * rows, width), BF16),
            pltpu.VMEM((window, 8, rows), F32),
            pltpu.VMEM((rows, window * rows), F32),
        ],
        compiler_params=pltpu.CompilerParams(vmem_limit_bytes=16 * MIB),
        cost_estimate=pl.CostEstimate(
            flops=4 * rows * heads * window * rows * width,
            bytes_accessed=4 * rows * heads * width,
            transcendentals=rows * heads * window * rows,
        ),
    )(info, query.reshape(rows * heads, width), *blocks)


def project_kernel(rows_ref, weight_ref, *outs):
    product = jnp.dot(rows_ref[...], weight_ref[...], preferred_element_type=F32).astype(BF16)
    quarter = product.shape[0] // 4
    for s, out in enumerate(outs):
        out[...] = product[s * quarter : (s + 1) * quarter]


def project(rows, weight):
    count, depth = rows.shape
    columns = weight.shape[1]
    tile = 512
    quarter = count // 4
    return pl.pallas_call(
        project_kernel,
        grid=(columns // tile,),
        out_shape=[jax.ShapeDtypeStruct((quarter, columns), BF16)] * 4,
        in_specs=[
            pl.BlockSpec((count, depth), lambda i: (0, 0)),
            pl.BlockSpec((depth, tile), lambda i: (0, i)),
        ],
        out_specs=[pl.BlockSpec((quarter, tile), lambda i: (0, i))] * 4,
        compiler_params=pltpu.CompilerParams(vmem_limit_bytes=16 * MIB),
        cost_estimate=pl.CostEstimate(
            flops=2 * count * depth * columns,
            bytes_accessed=2 * depth * columns,
            transcendentals=0,
        ),
    )(rows, weight)


def reduce_line(parts):
    def swap(value, pairs):
        return lax.ppermute(value, "tp", pairs)

    first, second, third, kept = parts
    first_in = swap(first, OUTER)
    second_in = swap(second, OUTER)
    first_far = swap(first + first_in, INNER)
    second_far = swap(second + second_in, INNER)
    third_in = swap(third + first_far, OUTER)
    return kept + third_in + second_far


def shards_line(query_rows, key_rows, value_rows, doc_ids, out_weight):
    rows, heads, width = query_rows.shape
    columns = out_weight.shape[1]
    mine = lax.axis_index(("pipe", "ctx"))
    place = jnp.asarray(PLACE, jnp.int32)[lax.axis_index("tp")]
    window = 5
    packed = pack(key_rows, value_rows, doc_ids)
    blocks = [packed] + [
        lax.ppermute(packed, ("pipe", "ctx"), [(i, i ^ m) for i in range(8)]) for m in range(1, 8)
    ]
    other_query = lax.ppermute(query_rows, "ctx", [(0, 1), (1, 0)])
    halves = []
    for asked, query in ((mine, query_rows), (mine ^ 1, other_query)):
        info = jnp.concatenate([jnp.stack([mine, asked]).astype(jnp.int32), place])
        rows_now = attend(info, query, blocks, window)
        halves.append(reduce_line(project(rows_now, out_weight)))
    at_first = lax.axis_index("ctx") == 0
    own, other = halves
    both = jnp.stack([jnp.where(at_first, own, other), jnp.where(at_first, other, own)])
    return both.reshape(1, 2, 1, rows // 4, columns)


def shards_any(query_rows, key_rows, value_rows, doc_ids, out_weight):
    rows, heads, width = query_rows.shape
    kv_local = key_rows.shape[1]
    group = heads // kv_local
    mine = lax.axis_index(("pipe", "ctx"))
    marks = doc_ids.astype(BF16)
    keys = lax.all_gather(key_rows, ("pipe", "ctx"), axis=0, tiled=True)
    values = lax.all_gather(value_rows, ("pipe", "ctx"), axis=0, tiled=True)
    key_doc = lax.all_gather(marks, ("pipe", "ctx"), axis=0, tiled=True).astype(jnp.int32)
    key_pos = jnp.arange(keys.shape[0], dtype=jnp.int32)
    half = rows // 2
    done = []
    for part in range(2):
        at = slice(part * half, (part + 1) * half)
        query = query_rows[at].reshape(half, kv_local, group, width)
        query_pos = mine * rows + part * half + jnp.arange(half, dtype=jnp.int32)
        scores = jnp.einsum("qjgd,kjd->qjgk", query, keys, preferred_element_type=F32)
        scores = scores * width**-0.5
        allowed = (key_pos[None, :] <= query_pos[:, None]) & (
            key_doc[None, :] == doc_ids[at][:, None]
        )
        allowed = allowed[:, None, None, :]
        masked = jnp.where(allowed, scores, -1e30)
        peak = jnp.max(masked, axis=3, keepdims=True)
        weights = jnp.where(allowed, jnp.exp(scores - peak), 0.0)
        total = jnp.sum(weights, axis=3)
        summed = jnp.einsum(
            "qjgk,kjd->qjgd", weights.astype(BF16), values, preferred_element_type=F32
        )
        done.append((summed / total[..., None]).astype(BF16).reshape(half, heads * width))
    flat = jnp.concatenate(done, axis=0)
    tp_size, ctx_size = lax.axis_size("tp"), lax.axis_size("ctx")
    quarter, columns = rows // tp_size, out_weight.shape[1]
    partial = jnp.dot(
        lax.all_gather(flat, "ctx", axis=0, tiled=True), out_weight, preferred_element_type=F32
    )
    partial = partial.reshape(ctx_size, tp_size, quarter, columns)
    summed = lax.psum_scatter(partial.astype(BF16), "tp", scatter_dimension=1, tiled=True)
    return summed.reshape(1, ctx_size, 1, quarter, columns)


def solution(mesh):
    sizes = dict(mesh.shape)
    on_line = sizes["tp"] == 4 and sizes["ctx"] == 2 and sizes["pipe"] == 4
    return jax.shard_map(
        shards_line if on_line else shards_any,
        mesh=mesh,
        in_specs=(
            P(("pipe", "ctx"), "tp", None),
            P(("pipe", "ctx"), "tp", None),
            P(("pipe", "ctx"), "tp", None),
            P(("pipe", "ctx")),
            P("tp", "ctx"),
        ),
        out_specs=P("pipe", None, "tp", None, "ctx"),
        check_vma=False,
    )
```

```python
import functools

import jax
import jax.numpy as jnp
from jax import lax
from jax.experimental import pallas as pl
from jax.experimental.pallas import tpu as pltpu
from jax.sharding import PartitionSpec as P

BF16 = jnp.bfloat16
F32 = jnp.float32
LOG2E = 1.4426950408889634
MIB = 1 << 20

WEIGHT_CUTS = 4
OUTER = ((0, 1), (1, 0), (2, 3), (3, 2))
INNER = ((1, 2), (2, 1))


def pin(value):
    return pltpu.with_memory_space_constraint(value, pltpu.HBM)


def pack_kernel(key_ref, value_ref, doc_ref, out_ref, marks, sems):
    rows = key_ref.shape[0]
    copies = [
        pltpu.make_async_copy(doc_ref, marks, sems.at[0]),
        pltpu.make_async_copy(key_ref, out_ref.at[pl.ds(0, rows)], sems.at[1]),
        pltpu.make_async_copy(value_ref, out_ref.at[pl.ds(rows, rows)], sems.at[2]),
    ]
    for copy in copies:
        copy.start()
    copies[0].wait()
    out_ref[2 * rows :] = jnp.broadcast_to(marks[...].astype(F32), (16, rows)).astype(BF16)
    copies[1].wait()
    copies[2].wait()


def pack(key_rows, value_rows, doc_ids):
    rows, _, width = key_rows.shape
    return pl.pallas_call(
        pack_kernel,
        out_shape=jax.ShapeDtypeStruct((2 * rows + 16, width), BF16),
        in_specs=[pl.BlockSpec(memory_space=pltpu.HBM)] * 3,
        out_specs=pl.BlockSpec(memory_space=pltpu.VMEM),
        scratch_shapes=[pltpu.VMEM((1, rows), jnp.int32), pltpu.SemaphoreType.DMA((3,))],
        compiler_params=pltpu.CompilerParams(vmem_limit_bytes=40 * MIB),
    )(
        *(
            pin(value)
            for value in (
                key_rows.reshape(rows, width),
                value_rows.reshape(rows, width),
                doc_ids.reshape(1, rows),
            )
        )
    )


def block_kernel(window, heads, flip, query_ref, weight_ref, *refs):
    blocks, outs = refs[:8], refs[8:-10]
    query_in, wide, query_all, keys, values, marks, bias, result, weight, sems = refs[-10:]
    rows, width = blocks[0].shape[0] // 2 - 8, blocks[0].shape[1]
    mine = lax.axis_index(("pipe", "ctx"))
    line = lax.axis_index("tp")
    asked = mine ^ flip
    columns = weight_ref.shape[1]
    tile = columns // WEIGHT_CUTS

    copies = [pltpu.make_async_copy(query_ref, query_in, sems.at[0])]
    for i in range(WEIGHT_CUTS):
        at = pl.ds(i * tile, tile)
        copies.append(pltpu.make_async_copy(weight_ref.at[:, at], weight.at[:, at], sems.at[1 + i]))
    for copy in copies:
        copy.start()

    keys[...] = jnp.zeros_like(keys)
    values[...] = jnp.zeros_like(values)
    marks[...] = jnp.full_like(marks, -1.0)
    for m in range(8):
        slot = (mine ^ m) - asked + window - 1

        @pl.when((slot >= 0) & (slot < window))
        def _(m=m, slot=slot):
            at = pl.ds(pl.multiple_of(slot * rows, rows), rows)
            keys[at, :] = blocks[m][:rows]
            values[at, :] = blocks[m][rows : 2 * rows]
            marks[slot] = blocks[m][2 * rows :].astype(F32)[:8]

    own = jnp.transpose(jnp.broadcast_to(marks[window - 1][:1], (rows, rows)))
    for s in range(window):
        allowed = own == marks[s][:1]
        if s == window - 1:
            at_row = lax.broadcasted_iota(jnp.int32, (rows, rows), 0)
            at_col = lax.broadcasted_iota(jnp.int32, (rows, rows), 1)
            allowed = allowed & (at_col <= at_row)
        bias[:, s * rows : (s + 1) * rows] = jnp.where(allowed, 0.0, -1e30)

    copies[0].wait()
    wide[...] = query_in[...].astype(F32)
    for h in range(heads):
        query_all[h * rows : (h + 1) * rows] = wide[pl.ds(h, rows, stride=heads), :].astype(BF16)

    quarter = rows // 4
    place = []
    for s in range(4):
        upper = jnp.where(s == line, 3, jnp.where(s > line, 3 - s, jnp.int32(2)))
        lower = jnp.where(s == line, 3, jnp.where(s < line, s, jnp.int32(2)))
        place.append(jnp.where(line < 2, upper, lower))

    factor = LOG2E * width**-0.5
    group = 4
    for g in range(heads // group):
        query = query_all[g * group * rows : (g + 1) * group * rows]
        scores = lax.dot_general(
            query, keys[...], (((1,), (1,)), ((), ())), preferred_element_type=F32
        )
        parts, totals = [], []
        for j in range(group):
            shifted = scores[j * rows : (j + 1) * rows] + bias[...]
            peak = jnp.max(shifted, axis=1, keepdims=True)
            weights = jnp.exp2((shifted - peak) * factor)
            totals.append(jnp.sum(weights, axis=1, keepdims=True))
            parts.append(weights.astype(BF16))
        summed = jnp.dot(
            jnp.concatenate(parts, axis=0), values[...], preferred_element_type=F32
        )
        for j in range(group):
            h = g * group + j
            done = (summed[j * rows : (j + 1) * rows] / totals[j]).astype(BF16)
            for s in range(4):
                at = pl.ds(pl.multiple_of(place[s] * quarter, quarter), quarter)
                result[at, h * width : (h + 1) * width] = done[s * quarter : (s + 1) * quarter]

    for i in range(WEIGHT_CUTS):
        copies[1 + i].wait()
        at = slice(i * tile, (i + 1) * tile)
        product = jnp.dot(result[...], weight[:, at], preferred_element_type=F32).astype(BF16)
        top = 0
        for out in outs:
            out[:, at] = product[top : top + out.shape[0]]
            top += out.shape[0]


def block(flip, query, blocks, weight, window, joined):
    rows, heads, width = query.shape
    depth, columns = weight.shape
    vmem = pl.BlockSpec(memory_space=pltpu.VMEM)
    quarter = rows // 4
    cuts = (2 * quarter, quarter, quarter) if joined else (quarter,) * 4
    place = pin if flip == 0 else lambda value: value
    return pl.pallas_call(
        functools.partial(block_kernel, window, heads, flip),
        out_shape=[jax.ShapeDtypeStruct((cut, columns), BF16) for cut in cuts],
        in_specs=[
            pl.BlockSpec(memory_space=pl.ANY),
            pl.BlockSpec(memory_space=pltpu.HBM),
        ]
        + [vmem] * 8,
        out_specs=[vmem] * len(cuts),
        scratch_shapes=[
            pltpu.VMEM((rows * heads, width), BF16),
            pltpu.VMEM((rows * heads, width), F32),
            pltpu.VMEM((rows * heads, width), BF16),
            pltpu.VMEM((window * rows, width), BF16),
            pltpu.VMEM((window * rows, width), BF16),
            pltpu.VMEM((window, 8, rows), F32),
            pltpu.VMEM((rows, window * rows), F32),
            pltpu.VMEM((rows, depth), BF16),
            pltpu.VMEM((depth, columns), BF16),
            pltpu.SemaphoreType.DMA((1 + WEIGHT_CUTS,)),
        ],
        compiler_params=pltpu.CompilerParams(vmem_limit_bytes=40 * MIB),
        cost_estimate=pl.CostEstimate(
            flops=4 * rows * heads * window * rows * width + 2 * rows * depth * columns,
            bytes_accessed=2 * depth * columns,
            transcendentals=rows * heads * window * rows,
        ),
    )(
        place(query.reshape(rows * heads, width)),
        pin(weight),
        *blocks,
    )


def swap(value, pairs):
    return lax.ppermute(value, "tp", pairs)


def shards_line(query_rows, key_rows, value_rows, doc_ids, out_weight):
    rows, heads, width = query_rows.shape
    columns = out_weight.shape[1]
    window = 5
    packed = pack(key_rows, value_rows, doc_ids)
    blocks = [packed] + [
        lax.ppermute(packed, ("pipe", "ctx"), [(i, i ^ m) for i in range(8)]) for m in range(1, 8)
    ]
    query_after, *_ = lax.optimization_barrier((query_rows, *blocks))
    other_query = lax.ppermute(query_after, "ctx", [(0, 1), (1, 0)])

    early, third, kept = block(0, query_rows, blocks, out_weight, window, True)
    late_first, late_second, late_third, late_kept = block(
        1, other_query, blocks, out_weight, window, False
    )
    early_in, late_first = lax.optimization_barrier((swap(early, OUTER), late_first))
    far = swap(early + early_in, INNER)
    quarter = rows // 4
    third_in = swap(third + far[:quarter], OUTER)
    late_far = swap(late_first + swap(late_first, OUTER), INNER)
    second_in, third_in = lax.optimization_barrier((swap(late_second, OUTER), third_in))
    late_near = swap(late_second + second_in, INNER)
    own = kept + third_in + far[quarter:]
    other = late_kept + swap(late_third + late_far, OUTER) + late_near
    at_first = lax.axis_index("ctx") == 0
    both = jnp.stack([jnp.where(at_first, own, other), jnp.where(at_first, other, own)])
    return both.reshape(1, 2, 1, rows // 4, columns)


def shards_any(query_rows, key_rows, value_rows, doc_ids, out_weight):
    rows, heads, width = query_rows.shape
    kv_local = key_rows.shape[1]
    group = heads // kv_local
    mine = lax.axis_index(("pipe", "ctx"))
    marks = doc_ids.astype(BF16)
    keys = lax.all_gather(key_rows, ("pipe", "ctx"), axis=0, tiled=True)
    values = lax.all_gather(value_rows, ("pipe", "ctx"), axis=0, tiled=True)
    key_doc = lax.all_gather(marks, ("pipe", "ctx"), axis=0, tiled=True).astype(jnp.int32)
    key_pos = jnp.arange(keys.shape[0], dtype=jnp.int32)
    half = rows // 2
    done = []
    for part in range(2):
        at = slice(part * half, (part + 1) * half)
        query = query_rows[at].reshape(half, kv_local, group, width)
        query_pos = mine * rows + part * half + jnp.arange(half, dtype=jnp.int32)
        scores = jnp.einsum("qjgd,kjd->qjgk", query, keys, preferred_element_type=F32)
        scores = scores * width**-0.5
        allowed = (key_pos[None, :] <= query_pos[:, None]) & (
            key_doc[None, :] == doc_ids[at][:, None]
        )
        allowed = allowed[:, None, None, :]
        masked = jnp.where(allowed, scores, -1e30)
        peak = jnp.max(masked, axis=3, keepdims=True)
        weights = jnp.where(allowed, jnp.exp(scores - peak), 0.0)
        total = jnp.sum(weights, axis=3)
        summed = jnp.einsum(
            "qjgk,kjd->qjgd", weights.astype(BF16), values, preferred_element_type=F32
        )
        done.append((summed / total[..., None]).astype(BF16).reshape(half, heads * width))
    flat = jnp.concatenate(done, axis=0)
    tp_size, ctx_size = lax.axis_size("tp"), lax.axis_size("ctx")
    quarter, columns = rows // tp_size, out_weight.shape[1]
    partial = jnp.dot(
        lax.all_gather(flat, "ctx", axis=0, tiled=True), out_weight, preferred_element_type=F32
    )
    partial = partial.reshape(ctx_size, tp_size, quarter, columns)
    summed = lax.psum_scatter(partial.astype(BF16), "tp", scatter_dimension=1, tiled=True)
    return summed.reshape(1, ctx_size, 1, quarter, columns)


def solution(mesh):
    sizes = dict(mesh.shape)
    on_line = sizes["tp"] == 4 and sizes["ctx"] == 2 and sizes["pipe"] == 4
    return jax.shard_map(
        shards_line if on_line else shards_any,
        mesh=mesh,
        in_specs=(
            P(("pipe", "ctx"), "tp", None),
            P(("pipe", "ctx"), "tp", None),
            P(("pipe", "ctx"), "tp", None),
            P(("pipe", "ctx")),
            P("tp", "ctx"),
        ),
        out_specs=P("pipe", None, "tp", None, "ctx"),
        check_vma=False,
    )
```

```python
import functools

import jax
import jax.numpy as jnp
from jax import lax
from jax.experimental import pallas as pl
from jax.experimental.pallas import tpu as pltpu
from jax.sharding import PartitionSpec as P

BF16 = jnp.bfloat16
F32 = jnp.float32
LOG2E = 1.4426950408889634
MIB = 1 << 20

WEIGHT_CUTS = 4
OUTER = ((0, 1), (1, 0), (2, 3), (3, 2))
INNER = tuple(
    (p * 8 + c * 4 + t, p * 8 + c * 4 + 3 - t if t in (1, 2) else (p ^ 1) * 8 + c * 4 + t)
    for p in range(4)
    for c in range(2)
    for t in range(4)
)


def pin(value):
    return pltpu.with_memory_space_constraint(value, pltpu.HBM)


def pack_kernel(key_ref, value_ref, doc_ref, out_ref, marks, sems):
    rows = key_ref.shape[0]
    copies = [
        pltpu.make_async_copy(doc_ref, marks, sems.at[0]),
        pltpu.make_async_copy(key_ref, out_ref.at[pl.ds(0, rows)], sems.at[1]),
        pltpu.make_async_copy(value_ref, out_ref.at[pl.ds(rows, rows)], sems.at[2]),
    ]
    for copy in copies:
        copy.start()
    copies[0].wait()
    out_ref[2 * rows :] = jnp.broadcast_to(marks[...].astype(F32), (16, rows)).astype(BF16)
    copies[1].wait()
    copies[2].wait()


def pack(key_rows, value_rows, doc_ids):
    rows, _, width = key_rows.shape
    return pl.pallas_call(
        pack_kernel,
        out_shape=jax.ShapeDtypeStruct((2 * rows + 16, width), BF16),
        in_specs=[pl.BlockSpec(memory_space=pltpu.HBM)] * 3,
        out_specs=pl.BlockSpec(memory_space=pltpu.VMEM),
        scratch_shapes=[pltpu.VMEM((1, rows), jnp.int32), pltpu.SemaphoreType.DMA((3,))],
        compiler_params=pltpu.CompilerParams(vmem_limit_bytes=24 * MIB),
    )(
        *(
            pin(value)
            for value in (
                key_rows.reshape(rows, width),
                value_rows.reshape(rows, width),
                doc_ids.reshape(1, rows),
            )
        )
    )


def leaving(line):
    upper = line < 2
    inside = (line == 1) | (line == 2)
    return (
        jnp.where(upper, 3, 0),
        jnp.where(upper, 2, 1),
        jnp.where(inside, jnp.where(upper, 0, 3), jnp.where(upper, 1, 2)),
        line,
    )


def attend(window, heads, shards, query_all, blocks, scratch, result):
    keys, values, marks, own, bias = scratch
    rows, width = blocks[0].shape[0] // 2 - 8, blocks[0].shape[1]
    quarter = rows // 4
    half = 2 * quarter
    mine = lax.axis_index(("pipe", "ctx"))

    keys[...] = jnp.zeros_like(keys)
    values[...] = jnp.zeros_like(values)
    marks[...] = jnp.full_like(marks, -1.0)
    for m in range(8):
        slot = (mine ^ m) - mine + window - 1

        @pl.when((slot >= 0) & (slot < window))
        def _(m=m, slot=slot):
            at = pl.ds(pl.multiple_of(slot * rows, rows), rows)
            keys[at, :] = blocks[m][:rows]
            values[at, :] = blocks[m][rows : 2 * rows]
            marks[slot] = blocks[m][2 * rows :].astype(F32)[:8]

    own[...] = jnp.transpose(jnp.broadcast_to(marks[window - 1][:1], (rows, rows)))
    for i, shard in enumerate(shards):
        start = pl.multiple_of(shard * quarter, quarter)
        here = own[pl.ds(start, quarter), :]
        for s in range(window):
            allowed = here == marks[s][:1]
            if s == window - 1:
                at_row = lax.broadcasted_iota(jnp.int32, (quarter, rows), 0) + start
                at_col = lax.broadcasted_iota(jnp.int32, (quarter, rows), 1)
                allowed = allowed & (at_col <= at_row)
            bias[i * quarter : (i + 1) * quarter, s * rows : (s + 1) * rows] = jnp.where(
                allowed, 0.0, -1e30
            )

    factor = LOG2E * width**-0.5
    group = 8
    for g in range(heads // group):
        query = query_all[g * group * half : (g + 1) * group * half]
        scores = lax.dot_general(
            query, keys[...], (((1,), (1,)), ((), ())), preferred_element_type=F32
        )
        parts, totals = [], []
        for j in range(group):
            shifted = scores[j * half : (j + 1) * half] + bias[...]
            peak = jnp.max(shifted, axis=1, keepdims=True)
            weights = jnp.exp2((shifted - peak) * factor)
            totals.append(jnp.sum(weights, axis=1, keepdims=True))
            parts.append(weights.astype(BF16))
        summed = jnp.dot(
            jnp.concatenate(parts, axis=0), values[...], preferred_element_type=F32
        )
        for j in range(group):
            h = g * group + j
            done = (summed[j * half : (j + 1) * half] / totals[j]).astype(BF16)
            result[:, h * width : (h + 1) * width] = done


def project(rows, weight, outs):
    tile = weight.shape[1] // 4
    for i in range(4):
        at = slice(i * tile, (i + 1) * tile)
        product = jnp.dot(rows, weight[:, at], preferred_element_type=F32).astype(BF16)
        top = 0
        for out in outs:
            out[:, at] = product[top : top + out.shape[0]]
            top += out.shape[0]


def filled(rows):
    return jnp.concatenate([rows, jnp.zeros_like(rows)], axis=0)


def far_kernel(window, heads, query_ref, weight_ref, *refs):
    blocks, (rows_out, first, second), scratch = refs[:8], refs[8:11], refs[11:]
    shards = leaving(lax.axis_index("tp"))[:2]
    attend(window, heads, shards, query_ref, blocks, scratch, rows_out)
    project(filled(rows_out[...]), weight_ref, (first, second))


def near_kernel(window, heads, query_ref, *refs):
    shards = leaving(lax.axis_index("tp"))[2:]
    attend(window, heads, shards, query_ref, refs[:8], refs[9:], refs[8])


def attention_call(query, blocks, window, weight=None):
    width = query.shape[1]
    rows = blocks[0].shape[0] // 2 - 8
    half = rows // 2
    heads = query.shape[0] // half
    vmem = pl.BlockSpec(memory_space=pltpu.VMEM)
    scratch = [
        pltpu.VMEM((window * rows, width), BF16),
        pltpu.VMEM((window * rows, width), BF16),
        pltpu.VMEM((window, 8, rows), F32),
        pltpu.VMEM((rows, rows), F32),
        pltpu.VMEM((half, window * rows), F32),
    ]
    flops = 4 * half * heads * window * rows * width
    outs = [jax.ShapeDtypeStruct((half, heads * width), BF16)]
    given, specs = [query], [vmem]
    kernel = near_kernel
    if weight is not None:
        depth, columns = weight.shape
        outs += [jax.ShapeDtypeStruct((half // 2, columns), BF16)] * 2
        given.append(pltpu.with_memory_space_constraint(weight, pltpu.VMEM))
        specs.append(vmem)
        flops += 2 * half * depth * columns
        kernel = far_kernel
    return pl.pallas_call(
        functools.partial(kernel, window, heads),
        out_shape=outs,
        in_specs=specs + [vmem] * 8,
        out_specs=[vmem] * len(outs),
        scratch_shapes=scratch,
        compiler_params=pltpu.CompilerParams(vmem_limit_bytes=24 * MIB),
        cost_estimate=pl.CostEstimate(
            flops=flops, bytes_accessed=MIB, transcendentals=half * heads * window * rows
        ),
    )(*given, *blocks)


def project_kernel(count, *refs):
    weight_ref = refs[count]
    rows = [ref[...] for ref in refs[:count]]
    rows = filled(rows[0]) if count == 1 else jnp.concatenate(rows, axis=0)
    project(rows, weight_ref, refs[count + 1 :])


def project_call(parts, weight):
    depth, columns = weight.shape
    half = parts[0].shape[0]
    vmem = pl.BlockSpec(memory_space=pltpu.VMEM)
    outs = [jax.ShapeDtypeStruct((half // 2, columns), BF16)] * (2 * len(parts))
    return pl.pallas_call(
        functools.partial(project_kernel, len(parts)),
        out_shape=outs,
        in_specs=[vmem] * (len(parts) + 1),
        out_specs=[vmem] * len(outs),
        compiler_params=pltpu.CompilerParams(vmem_limit_bytes=24 * MIB),
        cost_estimate=pl.CostEstimate(
            flops=2 * half * len(parts) * depth * columns,
            bytes_accessed=2 * depth * columns,
            transcendentals=0,
        ),
    )(*parts, pltpu.with_memory_space_constraint(weight, pltpu.VMEM))


def load_kernel(heads, weight_ref, query_ref, out_ref, far_ref, near_ref, query_in, wide, sems):
    depth = weight_ref.shape[0] // WEIGHT_CUTS
    size = query_ref.shape[0] // 4
    half = 2 * size // heads
    copies = [
        pltpu.make_async_copy(
            query_ref.at[pl.ds(pl.multiple_of(shard * size, size), size)],
            query_in.at[pl.ds(i * size, size)],
            sems.at[i],
        )
        for i, shard in enumerate(leaving(lax.axis_index("tp")))
    ]
    for i in range(WEIGHT_CUTS):
        at = pl.ds(i * depth, depth)
        copies.append(pltpu.make_async_copy(weight_ref.at[at], out_ref.at[at], sems.at[4 + i]))
    for copy in copies:
        copy.start()
    for copy in copies[:4]:
        copy.wait()
    wide[...] = query_in[...].astype(F32)
    for part, ref in enumerate((far_ref, near_ref)):
        for h in range(heads):
            start = part * half * heads + h
            ref[h * half : (h + 1) * half] = wide[pl.ds(start, half, stride=heads), :].astype(BF16)
    for copy in copies[4:]:
        copy.wait()


def load(weight, query):
    rows, heads, width = query.shape
    hbm, vmem = pl.BlockSpec(memory_space=pltpu.HBM), pl.BlockSpec(memory_space=pltpu.VMEM)
    part = pltpu.VMEM((rows // 2 * heads, width), BF16)
    return pl.pallas_call(
        functools.partial(load_kernel, heads),
        out_shape=[pltpu.VMEM(weight.shape, weight.dtype), part, part],
        in_specs=[hbm, hbm],
        out_specs=[vmem] * 3,
        scratch_shapes=[
            pltpu.VMEM((rows * heads, width), BF16),
            pltpu.VMEM((rows * heads, width), F32),
            pltpu.SemaphoreType.DMA((4 + WEIGHT_CUTS,)),
        ],
        compiler_params=pltpu.CompilerParams(vmem_limit_bytes=24 * MIB),
        cost_estimate=pl.CostEstimate(flops=0, bytes_accessed=weight.size * 4, transcendentals=0),
    )(pin(weight), pin(query.reshape(rows * heads, width)))


def swap(value):
    return lax.ppermute(value, "tp", OUTER)


def swap_inner(value):
    return lax.ppermute(value, ("pipe", "ctx", "tp"), INNER)


def shards_line(query_rows, key_rows, value_rows, doc_ids, out_weight):
    rows, heads, width = query_rows.shape
    columns = out_weight.shape[1]
    window = 5
    packed = pack(key_rows, value_rows, doc_ids)

    def pair(value, m):
        return lax.ppermute(value, ("pipe", "ctx"), [(i, i ^ m) for i in range(8)])

    by_x, by_y, by_both = pair(packed, 4), pair(packed, 1), pair(packed, 5)
    by_core = pair(packed, 2)
    after = lax.optimization_barrier
    line = lax.axis_index("tp")
    weight_here, inside = after((out_weight, (line == 1) | (line == 2)))
    weight, far_query, near_query = load(weight_here, query_rows)
    by_x, by_both, by_y, weight = after((by_x, by_both, by_y, weight))
    blocks = [packed, by_y, by_core, pair(by_y, 2), by_x, by_both, pair(by_x, 2), pair(by_both, 2)]

    def trade(value):
        return lax.ppermute(value, "ctx", [(0, 1), (1, 0)])

    def passed(value):
        return jnp.where(inside, value, jnp.zeros_like(value))

    far_rows, first, second = attention_call(far_query, blocks, window, weight)
    near_query, far_rows = after((near_query, far_rows))
    (near_rows,) = attention_call(near_query, blocks, window)
    other_far, other_near = trade(far_rows), trade(near_rows)
    late_first, late_second = project_call([other_far], weight)
    third, kept, late_third, late_kept = project_call([near_rows, other_near], weight)

    far = swap_inner(first + swap(first))
    near = swap_inner(second + swap(second))
    late_far = swap_inner(late_first + swap(late_first))
    late_near = swap_inner(late_second + swap(late_second))
    own = kept + swap(third + passed(far)) + passed(near)
    other = late_kept + swap(late_third + passed(late_far)) + passed(late_near)
    quarter = rows // 4
    at_first = lax.axis_index("ctx") == 0
    both = jnp.stack([jnp.where(at_first, own, other), jnp.where(at_first, other, own)])
    return both.reshape(1, 2, 1, rows // 4, columns)


def shards_any(query_rows, key_rows, value_rows, doc_ids, out_weight):
    rows, heads, width = query_rows.shape
    kv_local = key_rows.shape[1]
    group = heads // kv_local
    mine = lax.axis_index(("pipe", "ctx"))
    marks = doc_ids.astype(BF16)
    keys = lax.all_gather(key_rows, ("pipe", "ctx"), axis=0, tiled=True)
    values = lax.all_gather(value_rows, ("pipe", "ctx"), axis=0, tiled=True)
    key_doc = lax.all_gather(marks, ("pipe", "ctx"), axis=0, tiled=True).astype(jnp.int32)
    key_pos = jnp.arange(keys.shape[0], dtype=jnp.int32)
    half = rows // 2
    done = []
    for part in range(2):
        at = slice(part * half, (part + 1) * half)
        query = query_rows[at].reshape(half, kv_local, group, width)
        query_pos = mine * rows + part * half + jnp.arange(half, dtype=jnp.int32)
        scores = jnp.einsum("qjgd,kjd->qjgk", query, keys, preferred_element_type=F32)
        scores = scores * width**-0.5
        allowed = (key_pos[None, :] <= query_pos[:, None]) & (
            key_doc[None, :] == doc_ids[at][:, None]
        )
        allowed = allowed[:, None, None, :]
        masked = jnp.where(allowed, scores, -1e30)
        peak = jnp.max(masked, axis=3, keepdims=True)
        weights = jnp.where(allowed, jnp.exp(scores - peak), 0.0)
        total = jnp.sum(weights, axis=3)
        summed = jnp.einsum(
            "qjgk,kjd->qjgd", weights.astype(BF16), values, preferred_element_type=F32
        )
        done.append((summed / total[..., None]).astype(BF16).reshape(half, heads * width))
    flat = jnp.concatenate(done, axis=0)
    tp_size, ctx_size = lax.axis_size("tp"), lax.axis_size("ctx")
    quarter, columns = rows // tp_size, out_weight.shape[1]
    partial = jnp.dot(
        lax.all_gather(flat, "ctx", axis=0, tiled=True), out_weight, preferred_element_type=F32
    )
    partial = partial.reshape(ctx_size, tp_size, quarter, columns)
    summed = lax.psum_scatter(partial.astype(BF16), "tp", scatter_dimension=1, tiled=True)
    return summed.reshape(1, ctx_size, 1, quarter, columns)


def solution(mesh):
    sizes = dict(mesh.shape)
    on_line = sizes["tp"] == 4 and sizes["ctx"] == 2 and sizes["pipe"] == 4
    return jax.shard_map(
        shards_line if on_line else shards_any,
        mesh=mesh,
        in_specs=(
            P(("pipe", "ctx"), "tp", None),
            P(("pipe", "ctx"), "tp", None),
            P(("pipe", "ctx"), "tp", None),
            P(("pipe", "ctx")),
            P("tp", "ctx"),
        ),
        out_specs=P("pipe", None, "tp", None, "ctx"),
        check_vma=False,
    )
```

```python
import functools

import jax
import jax.numpy as jnp
from jax import lax
from jax.experimental import pallas as pl
from jax.experimental.pallas import tpu as pltpu
from jax.sharding import PartitionSpec as P

BF16 = jnp.bfloat16
F32 = jnp.float32
LOG2E = 1.4426950408889634
MIB = 1 << 20

WEIGHT_CUTS = 4
OUTER = ((0, 1), (1, 0), (2, 3), (3, 2))
INNER = tuple(
    (p * 8 + c * 4 + t, p * 8 + c * 4 + 3 - t if t in (1, 2) else (p ^ 1) * 8 + c * 4 + t)
    for p in range(4)
    for c in range(2)
    for t in range(4)
)


def pin(value):
    return pltpu.with_memory_space_constraint(value, pltpu.HBM)


def pack_kernel(key_ref, value_ref, doc_ref, out_ref, marks, sems):
    rows = key_ref.shape[0]
    copies = [
        pltpu.make_async_copy(doc_ref, marks, sems.at[0]),
        pltpu.make_async_copy(key_ref, out_ref.at[pl.ds(0, rows)], sems.at[1]),
        pltpu.make_async_copy(value_ref, out_ref.at[pl.ds(rows, rows)], sems.at[2]),
    ]
    for copy in copies:
        copy.start()
    copies[0].wait()
    out_ref[2 * rows :] = jnp.broadcast_to(marks[...].astype(F32), (16, rows)).astype(BF16)
    copies[1].wait()
    copies[2].wait()


def pack(key_rows, value_rows, doc_ids):
    rows, _, width = key_rows.shape
    return pl.pallas_call(
        pack_kernel,
        out_shape=jax.ShapeDtypeStruct((2 * rows + 16, width), BF16),
        in_specs=[pl.BlockSpec(memory_space=pltpu.HBM)] * 3,
        out_specs=pl.BlockSpec(memory_space=pltpu.VMEM),
        scratch_shapes=[pltpu.VMEM((1, rows), jnp.int32), pltpu.SemaphoreType.DMA((3,))],
        compiler_params=pltpu.CompilerParams(vmem_limit_bytes=24 * MIB),
    )(
        *(
            pin(value)
            for value in (
                key_rows.reshape(rows, width),
                value_rows.reshape(rows, width),
                doc_ids.reshape(1, rows),
            )
        )
    )


def leaving(line):
    upper = line < 2
    inside = (line == 1) | (line == 2)
    return (
        jnp.where(upper, 3, 0),
        jnp.where(upper, 2, 1),
        jnp.where(inside, jnp.where(upper, 0, 3), jnp.where(upper, 1, 2)),
        line,
    )


def attend(window, heads, shards, query_all, blocks, scratch, result):
    keys, values, marks, own, bias = scratch
    rows, width = blocks[0].shape[0] // 2 - 8, blocks[0].shape[1]
    quarter = rows // 4
    half = 2 * quarter
    mine = lax.axis_index(("pipe", "ctx"))

    keys[...] = jnp.zeros_like(keys)
    values[...] = jnp.zeros_like(values)
    marks[...] = jnp.full_like(marks, -1.0)
    for m in range(8):
        slot = (mine ^ m) - mine + window - 1

        @pl.when((slot >= 0) & (slot < window))
        def _(m=m, slot=slot):
            at = pl.ds(pl.multiple_of(slot * rows, rows), rows)
            keys[at, :] = blocks[m][:rows]
            values[at, :] = blocks[m][rows : 2 * rows]
            marks[slot] = blocks[m][2 * rows :].astype(F32)[:8]

    own[...] = jnp.transpose(jnp.broadcast_to(marks[window - 1][:1], (rows, rows)))
    for i, shard in enumerate(shards):
        start = pl.multiple_of(shard * quarter, quarter)
        here = own[pl.ds(start, quarter), :]
        for s in range(window):
            allowed = here == marks[s][:1]
            if s == window - 1:
                at_row = lax.broadcasted_iota(jnp.int32, (quarter, rows), 0) + start
                at_col = lax.broadcasted_iota(jnp.int32, (quarter, rows), 1)
                allowed = allowed & (at_col <= at_row)
            bias[i * quarter : (i + 1) * quarter, s * rows : (s + 1) * rows] = jnp.where(
                allowed, 0.0, -1e30
            )

    factor = LOG2E * width**-0.5
    group = 8
    for g in range(heads // group):
        query = query_all[g * group * half : (g + 1) * group * half]
        scores = lax.dot_general(
            query, keys[...], (((1,), (1,)), ((), ())), preferred_element_type=F32
        )
        parts, totals = [], []
        for j in range(group):
            shifted = scores[j * half : (j + 1) * half] + bias[...]
            peak = jnp.max(shifted, axis=1, keepdims=True)
            weights = jnp.exp2((shifted - peak) * factor)
            totals.append(jnp.sum(weights, axis=1, keepdims=True))
            parts.append(weights.astype(BF16))
        summed = jnp.dot(
            jnp.concatenate(parts, axis=0), values[...], preferred_element_type=F32
        )
        for j in range(group):
            h = g * group + j
            done = (summed[j * half : (j + 1) * half] / totals[j]).astype(BF16)
            result[:, h * width : (h + 1) * width] = done


def project(rows, weight, outs, left):
    tile = outs[0].shape[1] // 4
    for i in range(weight.shape[1] // tile):
        part = weight[:, i * tile : (i + 1) * tile]
        product = jnp.dot(rows, part, preferred_element_type=F32).astype(BF16)
        at, top = slice(left + i * tile, left + (i + 1) * tile), 0
        for out in outs:
            out[:, at] = product[top : top + out.shape[0]]
            top += out.shape[0]


def filled(rows):
    return jnp.concatenate([rows, jnp.zeros_like(rows)], axis=0)


def far_kernel(window, heads, query_ref, wide_ref, weight_ref, *refs):
    blocks, (rows_out, first, second, rest_ref) = refs[:8], refs[8:12]
    scratch, sems = refs[12:-1], refs[-1]
    copies = pieces(weight_ref, rest_ref, wide_ref.shape[1], WEIGHT_CUTS, sems)
    for copy in copies:
        copy.start()
    shards = leaving(lax.axis_index("tp"))[:2]
    attend(window, heads, shards, query_ref, blocks, scratch, rows_out)
    rows = filled(rows_out[...])
    project(rows, wide_ref, (first, second), 0)
    for copy in copies:
        copy.wait()
    project(rows, rest_ref, (first, second), wide_ref.shape[1])


def near_kernel(window, heads, query_ref, *refs):
    shards = leaving(lax.axis_index("tp"))[2:]
    attend(window, heads, shards, query_ref, refs[:8], refs[9:], refs[8])


def attention_call(query, blocks, window, weight=None):
    width = query.shape[1]
    rows = blocks[0].shape[0] // 2 - 8
    half = rows // 2
    heads = query.shape[0] // half
    vmem = pl.BlockSpec(memory_space=pltpu.VMEM)
    scratch = [
        pltpu.VMEM((window * rows, width), BF16),
        pltpu.VMEM((window * rows, width), BF16),
        pltpu.VMEM((window, 8, rows), F32),
        pltpu.VMEM((rows, rows), F32),
        pltpu.VMEM((half, window * rows), F32),
    ]
    flops = 4 * half * heads * window * rows * width
    outs = [jax.ShapeDtypeStruct((half, heads * width), BF16)]
    given, specs = [query], [vmem]
    kernel = near_kernel
    if weight is not None:
        (depth, columns), loaded = weight[1].shape, weight[0].shape[1]
        outs += [jax.ShapeDtypeStruct((half // 2, columns), BF16)] * 2
        outs.append(pltpu.VMEM((depth, columns - loaded), BF16))
        given += [weight[0], pin(weight[1])]
        specs += [vmem, pl.BlockSpec(memory_space=pltpu.HBM)]
        scratch.append(pltpu.SemaphoreType.DMA((WEIGHT_CUTS,)))
        flops += 2 * half * depth * columns
        kernel = far_kernel
    return pl.pallas_call(
        functools.partial(kernel, window, heads),
        out_shape=outs,
        in_specs=specs + [vmem] * 8,
        out_specs=[vmem] * len(outs),
        scratch_shapes=scratch,
        compiler_params=pltpu.CompilerParams(vmem_limit_bytes=24 * MIB),
        cost_estimate=pl.CostEstimate(
            flops=flops, bytes_accessed=MIB, transcendentals=half * heads * window * rows
        ),
    )(*given, *blocks)


def project_kernel(count, *refs):
    rows = [ref[...] for ref in refs[:count]]
    rows = filled(rows[0]) if count == 1 else jnp.concatenate(rows, axis=0)
    wide_ref, rest_ref, *outs = refs[count:]
    project(rows, wide_ref, outs, 0)
    project(rows, rest_ref, outs, wide_ref.shape[1])


def project_call(parts, weights):
    depth = parts[0].shape[1]
    columns = weights[0].shape[1] + weights[1].shape[1]
    half = parts[0].shape[0]
    vmem = pl.BlockSpec(memory_space=pltpu.VMEM)
    outs = [jax.ShapeDtypeStruct((half // 2, columns), BF16)] * (2 * len(parts))
    return pl.pallas_call(
        functools.partial(project_kernel, len(parts)),
        out_shape=outs,
        in_specs=[vmem] * (len(parts) + 2),
        out_specs=[vmem] * len(outs),
        compiler_params=pltpu.CompilerParams(vmem_limit_bytes=24 * MIB),
        cost_estimate=pl.CostEstimate(
            flops=2 * half * len(parts) * depth * columns,
            bytes_accessed=2 * depth * columns,
            transcendentals=0,
        ),
    )(*parts, *weights)


def pieces(weight_ref, part_ref, left, count, sems):
    depth, columns = part_ref.shape
    rows = depth // count
    return [
        pltpu.make_async_copy(
            weight_ref.at[pl.ds(i * rows, rows), pl.ds(left, columns)],
            part_ref.at[pl.ds(i * rows, rows)],
            sems.at[i],
        )
        for i in range(count)
    ]


def load_kernel(heads, weight_ref, query_ref, out_ref, far_ref, near_ref, query_in, wide, sems):
    size = query_ref.shape[0] // 4
    half = 2 * size // heads
    copies = [
        pltpu.make_async_copy(
            query_ref.at[pl.ds(pl.multiple_of(shard * size, size), size)],
            query_in.at[pl.ds(i * size, size)],
            sems.at[i],
        )
        for i, shard in enumerate(leaving(lax.axis_index("tp")))
    ]
    copies += pieces(weight_ref, out_ref, 0, WEIGHT_CUTS, sems.at[pl.ds(4, WEIGHT_CUTS)])
    for copy in copies:
        copy.start()
    for copy in copies[:4]:
        copy.wait()
    wide[...] = query_in[...].astype(F32)
    for part, ref in enumerate((far_ref, near_ref)):
        for h in range(heads):
            start = part * half * heads + h
            ref[h * half : (h + 1) * half] = wide[pl.ds(start, half, stride=heads), :].astype(BF16)
    for copy in copies[4:]:
        copy.wait()


def load(weight, query):
    rows, heads, width = query.shape
    depth, columns = weight.shape
    hbm, vmem = pl.BlockSpec(memory_space=pltpu.HBM), pl.BlockSpec(memory_space=pltpu.VMEM)
    part = pltpu.VMEM((rows // 2 * heads, width), BF16)
    return pl.pallas_call(
        functools.partial(load_kernel, heads),
        out_shape=[pltpu.VMEM((depth, columns * 3 // 4), BF16), part, part],
        in_specs=[hbm, hbm],
        out_specs=[vmem] * 3,
        scratch_shapes=[
            pltpu.VMEM((rows * heads, width), BF16),
            pltpu.VMEM((rows * heads, width), F32),
            pltpu.SemaphoreType.DMA((4 + WEIGHT_CUTS,)),
        ],
        compiler_params=pltpu.CompilerParams(vmem_limit_bytes=24 * MIB),
        cost_estimate=pl.CostEstimate(flops=0, bytes_accessed=weight.size * 4, transcendentals=0),
    )(pin(weight), pin(query.reshape(rows * heads, width)))


def swap(value):
    return lax.ppermute(value, "tp", OUTER)


def swap_inner(value):
    return lax.ppermute(value, ("pipe", "ctx", "tp"), INNER)


def shards_line(query_rows, key_rows, value_rows, doc_ids, out_weight):
    rows, heads, width = query_rows.shape
    columns = out_weight.shape[1]
    window = 5
    packed = pack(key_rows, value_rows, doc_ids)

    def pair(value, m):
        return lax.ppermute(value, ("pipe", "ctx"), [(i, i ^ m) for i in range(8)])

    by_x, by_y, by_both = pair(packed, 4), pair(packed, 1), pair(packed, 5)
    by_core = pair(packed, 2)
    after = lax.optimization_barrier
    line = lax.axis_index("tp")
    weight_here, inside = after((out_weight, (line == 1) | (line == 2)))
    weight, far_query, near_query = load(weight_here, query_rows)
    by_x, by_both, by_y, weight = after((by_x, by_both, by_y, weight))
    blocks = [packed, by_y, by_core, pair(by_y, 2), by_x, by_both, pair(by_x, 2), pair(by_both, 2)]

    def trade(value):
        return lax.ppermute(value, "ctx", [(0, 1), (1, 0)])

    def passed(value):
        return jnp.where(inside, value, jnp.zeros_like(value))

    far_rows, first, second, rest = attention_call(
        far_query, blocks, window, (weight, out_weight)
    )
    weights = (weight, rest)
    near_query, far_rows = after((near_query, far_rows))
    (near_rows,) = attention_call(near_query, blocks, window)
    other_far, other_near = trade(far_rows), trade(near_rows)
    first_sum = first + swap(first)
    far = swap_inner(first_sum)
    late_first, late_second = project_call([other_far], weights)
    other_near, far = after((other_near, far))
    third, kept, late_third, late_kept = project_call([near_rows, other_near], weights)
    near = swap_inner(second + swap(second))
    late_far = swap_inner(late_first + swap(late_first))
    late_near = swap_inner(late_second + swap(late_second))
    own = kept + swap(third + passed(far)) + passed(near)
    other = late_kept + swap(late_third + passed(late_far)) + passed(late_near)
    quarter = rows // 4
    at_first = lax.axis_index("ctx") == 0
    both = jnp.stack([jnp.where(at_first, own, other), jnp.where(at_first, other, own)])
    return both.reshape(1, 2, 1, rows // 4, columns)


def shards_any(query_rows, key_rows, value_rows, doc_ids, out_weight):
    rows, heads, width = query_rows.shape
    kv_local = key_rows.shape[1]
    group = heads // kv_local
    mine = lax.axis_index(("pipe", "ctx"))
    marks = doc_ids.astype(BF16)
    keys = lax.all_gather(key_rows, ("pipe", "ctx"), axis=0, tiled=True)
    values = lax.all_gather(value_rows, ("pipe", "ctx"), axis=0, tiled=True)
    key_doc = lax.all_gather(marks, ("pipe", "ctx"), axis=0, tiled=True).astype(jnp.int32)
    key_pos = jnp.arange(keys.shape[0], dtype=jnp.int32)
    half = rows // 2
    done = []
    for part in range(2):
        at = slice(part * half, (part + 1) * half)
        query = query_rows[at].reshape(half, kv_local, group, width)
        query_pos = mine * rows + part * half + jnp.arange(half, dtype=jnp.int32)
        scores = jnp.einsum("qjgd,kjd->qjgk", query, keys, preferred_element_type=F32)
        scores = scores * width**-0.5
        allowed = (key_pos[None, :] <= query_pos[:, None]) & (
            key_doc[None, :] == doc_ids[at][:, None]
        )
        allowed = allowed[:, None, None, :]
        masked = jnp.where(allowed, scores, -1e30)
        peak = jnp.max(masked, axis=3, keepdims=True)
        weights = jnp.where(allowed, jnp.exp(scores - peak), 0.0)
        total = jnp.sum(weights, axis=3)
        summed = jnp.einsum(
            "qjgk,kjd->qjgd", weights.astype(BF16), values, preferred_element_type=F32
        )
        done.append((summed / total[..., None]).astype(BF16).reshape(half, heads * width))
    flat = jnp.concatenate(done, axis=0)
    tp_size, ctx_size = lax.axis_size("tp"), lax.axis_size("ctx")
    quarter, columns = rows // tp_size, out_weight.shape[1]
    partial = jnp.dot(
        lax.all_gather(flat, "ctx", axis=0, tiled=True), out_weight, preferred_element_type=F32
    )
    partial = partial.reshape(ctx_size, tp_size, quarter, columns)
    summed = lax.psum_scatter(partial.astype(BF16), "tp", scatter_dimension=1, tiled=True)
    return summed.reshape(1, ctx_size, 1, quarter, columns)


def solution(mesh):
    sizes = dict(mesh.shape)
    on_line = sizes["tp"] == 4 and sizes["ctx"] == 2 and sizes["pipe"] == 4
    return jax.shard_map(
        shards_line if on_line else shards_any,
        mesh=mesh,
        in_specs=(
            P(("pipe", "ctx"), "tp", None),
            P(("pipe", "ctx"), "tp", None),
            P(("pipe", "ctx"), "tp", None),
            P(("pipe", "ctx")),
            P("tp", "ctx"),
        ),
        out_specs=P("pipe", None, "tp", None, "ctx"),
        check_vma=False,
    )
```

```python
import functools

import jax
import jax.numpy as jnp
from jax import lax
from jax.experimental import pallas as pl
from jax.experimental.pallas import tpu as pltpu
from jax.sharding import PartitionSpec as P

BF16 = jnp.bfloat16
F32 = jnp.float32
LOG2E = 1.4426950408889634
MIB = 1 << 20

WEIGHT_CUTS = 4
OUTER = ((0, 1), (1, 0), (2, 3), (3, 2))
INNER = tuple(
    (p * 8 + c * 4 + t, p * 8 + c * 4 + 3 - t if t in (1, 2) else (p ^ 1) * 8 + c * 4 + t)
    for p in range(4)
    for c in range(2)
    for t in range(4)
)


def pin(value):
    return pltpu.with_memory_space_constraint(value, pltpu.HBM)


def pack_kernel(key_ref, value_ref, doc_ref, out_ref, marks, sems):
    rows = key_ref.shape[0]
    copies = [
        pltpu.make_async_copy(doc_ref, marks, sems.at[0]),
        pltpu.make_async_copy(key_ref, out_ref.at[pl.ds(0, rows)], sems.at[1]),
        pltpu.make_async_copy(value_ref, out_ref.at[pl.ds(rows, rows)], sems.at[2]),
    ]
    for copy in copies:
        copy.start()
    copies[0].wait()
    out_ref[2 * rows :] = jnp.broadcast_to(marks[...].astype(F32), (16, rows)).astype(BF16)
    copies[1].wait()
    copies[2].wait()


def pack(key_rows, value_rows, doc_ids):
    rows, _, width = key_rows.shape
    return pl.pallas_call(
        pack_kernel,
        out_shape=jax.ShapeDtypeStruct((2 * rows + 16, width), BF16),
        in_specs=[pl.BlockSpec(memory_space=pltpu.HBM)] * 3,
        out_specs=pl.BlockSpec(memory_space=pltpu.VMEM),
        scratch_shapes=[pltpu.VMEM((1, rows), jnp.int32), pltpu.SemaphoreType.DMA((3,))],
        compiler_params=pltpu.CompilerParams(vmem_limit_bytes=24 * MIB),
    )(
        *(
            pin(value)
            for value in (
                key_rows.reshape(rows, width),
                value_rows.reshape(rows, width),
                doc_ids.reshape(1, rows),
            )
        )
    )


def leaving(line):
    upper = line < 2
    inside = (line == 1) | (line == 2)
    return (
        jnp.where(upper, 3, 0),
        jnp.where(upper, 2, 1),
        jnp.where(inside, jnp.where(upper, 0, 3), jnp.where(upper, 1, 2)),
        line,
    )


def attend(window, heads, shards, query_all, blocks, scratch, result):
    keys, values, marks, own, bias = scratch
    rows, width = blocks[0].shape[0] // 2 - 8, blocks[0].shape[1]
    quarter = rows // 4
    half = 2 * quarter
    mine = lax.axis_index(("pipe", "ctx"))

    keys[...] = jnp.zeros_like(keys)
    values[...] = jnp.zeros_like(values)
    marks[...] = jnp.full_like(marks, -1.0)
    for m in range(8):
        slot = (mine ^ m) - mine + window - 1

        @pl.when((slot >= 0) & (slot < window))
        def _(m=m, slot=slot):
            at = pl.ds(pl.multiple_of(slot * rows, rows), rows)
            keys[at, :] = blocks[m][:rows]
            values[at, :] = blocks[m][rows : 2 * rows]
            marks[slot] = blocks[m][2 * rows :].astype(F32)[:8]

    own[...] = jnp.transpose(jnp.broadcast_to(marks[window - 1][:1], (rows, rows)))
    for i, shard in enumerate(shards):
        start = pl.multiple_of(shard * quarter, quarter)
        here = own[pl.ds(start, quarter), :]
        for s in range(window):
            allowed = here == marks[s][:1]
            if s == window - 1:
                at_row = lax.broadcasted_iota(jnp.int32, (quarter, rows), 0) + start
                at_col = lax.broadcasted_iota(jnp.int32, (quarter, rows), 1)
                allowed = allowed & (at_col <= at_row)
            bias[i * quarter : (i + 1) * quarter, s * rows : (s + 1) * rows] = jnp.where(
                allowed, 0.0, -1e30
            )

    factor = LOG2E * width**-0.5
    group = 8
    for g in range(heads // group):
        query = query_all[g * group * half : (g + 1) * group * half]
        scores = lax.dot_general(
            query, keys[...], (((1,), (1,)), ((), ())), preferred_element_type=F32
        )
        parts, totals = [], []
        for j in range(group):
            shifted = scores[j * half : (j + 1) * half] + bias[...]
            peak = jnp.max(shifted, axis=1, keepdims=True)
            weights = jnp.exp2((shifted - peak) * factor)
            totals.append(jnp.sum(weights, axis=1, keepdims=True))
            parts.append(weights.astype(BF16))
        summed = jnp.dot(
            jnp.concatenate(parts, axis=0), values[...], preferred_element_type=F32
        )
        for j in range(group):
            h = g * group + j
            done = (summed[j * half : (j + 1) * half] / totals[j]).astype(BF16)
            result[:, h * width : (h + 1) * width] = done


def project(rows, weight, outs, left):
    tile = 1024 if weight.shape[1] % 1024 == 0 else weight.shape[1]
    for i in range(weight.shape[1] // tile):
        part = weight[:, i * tile : (i + 1) * tile]
        product = jnp.dot(rows, part, preferred_element_type=F32).astype(BF16)
        at, top = slice(left + i * tile, left + (i + 1) * tile), 0
        for out in outs:
            out[:, at] = product[top : top + out.shape[0]]
            top += out.shape[0]


def filled(rows):
    return jnp.concatenate([rows, jnp.zeros_like(rows)], axis=0)


def far_kernel(window, heads, query_ref, loaded_ref, weight_ref, *refs):
    blocks, (rows_out, early, part_ref) = refs[:8], refs[8:11]
    scratch, sems = refs[11:-1], refs[-1]
    copies = pieces(weight_ref, part_ref, loaded_ref.shape[1], WEIGHT_CUTS, sems)
    for copy in copies:
        copy.start()
    shards = leaving(lax.axis_index("tp"))[:2]
    attend(window, heads, shards, query_ref, blocks, scratch, rows_out)
    project(filled(rows_out[...]), loaded_ref, (early,), 0)
    for copy in copies:
        copy.wait()


def rest_kernel(left, rows_ref, loaded_ref, weight_ref, early, part_ref, sems):
    copies = pieces(weight_ref, part_ref, left, WEIGHT_CUTS, sems)
    for copy in copies:
        copy.start()
    rows = filled(rows_ref[...])
    project(rows, loaded_ref, (early,), 0)
    for copy in copies:
        copy.wait()
    project(rows, part_ref, (early,), loaded_ref.shape[1])


def rest_call(rows, loaded, weight):
    (half, depth), columns = rows.shape, weight.shape[1]
    vmem = pl.BlockSpec(memory_space=pltpu.VMEM)
    width = columns // 4
    return pl.pallas_call(
        functools.partial(rest_kernel, columns - width),
        out_shape=[
            jax.ShapeDtypeStruct((half, 2 * width), BF16),
            pltpu.VMEM((depth, width), BF16),
        ],
        in_specs=[vmem, vmem, pl.BlockSpec(memory_space=pltpu.HBM)],
        out_specs=[vmem, vmem],
        scratch_shapes=[pltpu.SemaphoreType.DMA((WEIGHT_CUTS,))],
        compiler_params=pltpu.CompilerParams(vmem_limit_bytes=24 * MIB),
        cost_estimate=pl.CostEstimate(
            flops=2 * half * depth * columns // 2, bytes_accessed=depth * columns, transcendentals=0
        ),
    )(rows, loaded, pin(weight))


def near_kernel(window, heads, query_ref, *refs):
    shards = leaving(lax.axis_index("tp"))[2:]
    attend(window, heads, shards, query_ref, refs[:8], refs[9:], refs[8])


def attention_call(query, blocks, window, weight=None):
    width = query.shape[1]
    rows = blocks[0].shape[0] // 2 - 8
    half = rows // 2
    heads = query.shape[0] // half
    vmem = pl.BlockSpec(memory_space=pltpu.VMEM)
    scratch = [
        pltpu.VMEM((window * rows, width), BF16),
        pltpu.VMEM((window * rows, width), BF16),
        pltpu.VMEM((window, 8, rows), F32),
        pltpu.VMEM((rows, rows), F32),
        pltpu.VMEM((half, window * rows), F32),
    ]
    flops = 4 * half * heads * window * rows * width
    outs = [jax.ShapeDtypeStruct((half, heads * width), BF16)]
    given, specs = [query], [vmem]
    kernel = near_kernel
    if weight is not None:
        (depth, columns), loaded = weight[1].shape, weight[0].shape[1]
        outs.append(jax.ShapeDtypeStruct((half, loaded), BF16))
        outs.append(pltpu.VMEM((depth, columns // 4), BF16))
        given += [weight[0], pin(weight[1])]
        specs += [vmem, pl.BlockSpec(memory_space=pltpu.HBM)]
        scratch.append(pltpu.SemaphoreType.DMA((WEIGHT_CUTS,)))
        flops += 2 * half * depth * loaded
        kernel = far_kernel
    return pl.pallas_call(
        functools.partial(kernel, window, heads),
        out_shape=outs,
        in_specs=specs + [vmem] * 8,
        out_specs=[vmem] * len(outs),
        scratch_shapes=scratch,
        compiler_params=pltpu.CompilerParams(vmem_limit_bytes=24 * MIB),
        cost_estimate=pl.CostEstimate(
            flops=flops, bytes_accessed=MIB, transcendentals=half * heads * window * rows
        ),
    )(*given, *blocks)


def project_kernel(count, *refs):
    rows = [ref[...] for ref in refs[:count]]
    rows = filled(rows[0]) if count == 1 else jnp.concatenate(rows, axis=0)
    left = 0
    for weight in refs[count : count + 3]:
        project(rows, weight, refs[count + 3 :], left)
        left += weight.shape[1]


def project_call(parts, weights):
    depth = parts[0].shape[1]
    columns = sum(weight.shape[1] for weight in weights)
    half = parts[0].shape[0]
    vmem = pl.BlockSpec(memory_space=pltpu.VMEM)
    outs = [jax.ShapeDtypeStruct((half // 2, columns), BF16)] * (2 * len(parts))
    return pl.pallas_call(
        functools.partial(project_kernel, len(parts)),
        out_shape=outs,
        in_specs=[vmem] * (len(parts) + 3),
        out_specs=[vmem] * len(outs),
        compiler_params=pltpu.CompilerParams(vmem_limit_bytes=24 * MIB),
        cost_estimate=pl.CostEstimate(
            flops=2 * half * len(parts) * depth * columns,
            bytes_accessed=2 * depth * columns,
            transcendentals=0,
        ),
    )(*parts, *weights)


def pieces(weight_ref, part_ref, left, count, sems):
    depth, columns = part_ref.shape
    rows = depth // count
    return [
        pltpu.make_async_copy(
            weight_ref.at[pl.ds(i * rows, rows), pl.ds(left, columns)],
            part_ref.at[pl.ds(i * rows, rows)],
            sems.at[i],
        )
        for i in range(count)
    ]


def load_kernel(heads, weight_ref, query_ref, out_ref, far_ref, near_ref, query_in, wide, sems):
    size = query_ref.shape[0] // 4
    half = 2 * size // heads
    copies = [
        pltpu.make_async_copy(
            query_ref.at[pl.ds(pl.multiple_of(shard * size, size), size)],
            query_in.at[pl.ds(i * size, size)],
            sems.at[i],
        )
        for i, shard in enumerate(leaving(lax.axis_index("tp")))
    ]
    copies += pieces(weight_ref, out_ref, 0, WEIGHT_CUTS, sems.at[pl.ds(4, WEIGHT_CUTS)])
    for copy in copies:
        copy.start()
    for copy in copies[:4]:
        copy.wait()
    wide[...] = query_in[...].astype(F32)
    for part, ref in enumerate((far_ref, near_ref)):
        for h in range(heads):
            start = part * half * heads + h
            ref[h * half : (h + 1) * half] = wide[pl.ds(start, half, stride=heads), :].astype(BF16)
    for copy in copies[4:]:
        copy.wait()


def load(weight, query):
    rows, heads, width = query.shape
    depth, columns = weight.shape
    hbm, vmem = pl.BlockSpec(memory_space=pltpu.HBM), pl.BlockSpec(memory_space=pltpu.VMEM)
    part = pltpu.VMEM((rows // 2 * heads, width), BF16)
    return pl.pallas_call(
        functools.partial(load_kernel, heads),
        out_shape=[pltpu.VMEM((depth, columns // 2), BF16), part, part],
        in_specs=[hbm, hbm],
        out_specs=[vmem] * 3,
        scratch_shapes=[
            pltpu.VMEM((rows * heads, width), BF16),
            pltpu.VMEM((rows * heads, width), F32),
            pltpu.SemaphoreType.DMA((4 + WEIGHT_CUTS,)),
        ],
        compiler_params=pltpu.CompilerParams(vmem_limit_bytes=24 * MIB),
        cost_estimate=pl.CostEstimate(flops=0, bytes_accessed=weight.size * 4, transcendentals=0),
    )(pin(weight), pin(query.reshape(rows * heads, width)))


def swap(value):
    return lax.ppermute(value, "tp", OUTER)


def swap_inner(value):
    return lax.ppermute(value, ("pipe", "ctx", "tp"), INNER)


def shards_line(query_rows, key_rows, value_rows, doc_ids, out_weight):
    rows, heads, width = query_rows.shape
    columns = out_weight.shape[1]
    window = 5
    packed = pack(key_rows, value_rows, doc_ids)

    def pair(value, m):
        return lax.ppermute(value, ("pipe", "ctx"), [(i, i ^ m) for i in range(8)])

    by_x, by_y, by_both = pair(packed, 4), pair(packed, 1), pair(packed, 5)
    by_core = pair(packed, 2)
    after = lax.optimization_barrier
    line = lax.axis_index("tp")
    weight_here, inside = after((out_weight, (line == 1) | (line == 2)))
    weight, far_query, near_query = load(weight_here, query_rows)
    by_x, by_both, by_y, weight = after((by_x, by_both, by_y, weight))
    blocks = [packed, by_y, by_core, pair(by_y, 2), by_x, by_both, pair(by_x, 2), pair(by_both, 2)]

    def trade(value):
        return lax.ppermute(value, "ctx", [(0, 1), (1, 0)])

    def passed(value):
        return jnp.where(inside, value, jnp.zeros_like(value))

    far_rows, early, part = attention_call(far_query, blocks, window, (weight, out_weight))
    early_in = swap(early)
    other_far = trade(far_rows)
    early_rest, last = rest_call(far_rows, part, out_weight)
    weights = (weight, part, last)
    near_query, early_rest = after((near_query, early_rest))
    (near_rows,) = attention_call(near_query, blocks, window)
    other_near = trade(near_rows)

    passed_on = swap_inner(early + early_in)
    late_first, late_second = project_call([other_far], weights)
    other_near, passed_on = after((other_near, passed_on))
    third, kept, late_third, late_kept = project_call([near_rows, other_near], weights)
    passed_rest = swap_inner(early_rest + swap(early_rest))
    late_in, third = after((swap(late_first), third))
    late_far = swap_inner(late_first + late_in)
    late_near = swap_inner(late_second + swap(late_second))
    both = passed(jnp.concatenate([passed_on, passed_rest], axis=1))
    quarter = rows // 4
    own = kept + swap(third + both[:quarter]) + both[quarter:]
    other = late_kept + swap(late_third + passed(late_far)) + passed(late_near)
    at_first = lax.axis_index("ctx") == 0
    both = jnp.stack([jnp.where(at_first, own, other), jnp.where(at_first, other, own)])
    return both.reshape(1, 2, 1, rows // 4, columns)


def shards_any(query_rows, key_rows, value_rows, doc_ids, out_weight):
    rows, heads, width = query_rows.shape
    kv_local = key_rows.shape[1]
    group = heads // kv_local
    mine = lax.axis_index(("pipe", "ctx"))
    marks = doc_ids.astype(BF16)
    keys = lax.all_gather(key_rows, ("pipe", "ctx"), axis=0, tiled=True)
    values = lax.all_gather(value_rows, ("pipe", "ctx"), axis=0, tiled=True)
    key_doc = lax.all_gather(marks, ("pipe", "ctx"), axis=0, tiled=True).astype(jnp.int32)
    key_pos = jnp.arange(keys.shape[0], dtype=jnp.int32)
    half = rows // 2
    done = []
    for part in range(2):
        at = slice(part * half, (part + 1) * half)
        query = query_rows[at].reshape(half, kv_local, group, width)
        query_pos = mine * rows + part * half + jnp.arange(half, dtype=jnp.int32)
        scores = jnp.einsum("qjgd,kjd->qjgk", query, keys, preferred_element_type=F32)
        scores = scores * width**-0.5
        allowed = (key_pos[None, :] <= query_pos[:, None]) & (
            key_doc[None, :] == doc_ids[at][:, None]
        )
        allowed = allowed[:, None, None, :]
        masked = jnp.where(allowed, scores, -1e30)
        peak = jnp.max(masked, axis=3, keepdims=True)
        weights = jnp.where(allowed, jnp.exp(scores - peak), 0.0)
        total = jnp.sum(weights, axis=3)
        summed = jnp.einsum(
            "qjgk,kjd->qjgd", weights.astype(BF16), values, preferred_element_type=F32
        )
        done.append((summed / total[..., None]).astype(BF16).reshape(half, heads * width))
    flat = jnp.concatenate(done, axis=0)
    tp_size, ctx_size = lax.axis_size("tp"), lax.axis_size("ctx")
    quarter, columns = rows // tp_size, out_weight.shape[1]
    partial = jnp.dot(
        lax.all_gather(flat, "ctx", axis=0, tiled=True), out_weight, preferred_element_type=F32
    )
    partial = partial.reshape(ctx_size, tp_size, quarter, columns)
    summed = lax.psum_scatter(partial.astype(BF16), "tp", scatter_dimension=1, tiled=True)
    return summed.reshape(1, ctx_size, 1, quarter, columns)


def solution(mesh):
    sizes = dict(mesh.shape)
    on_line = sizes["tp"] == 4 and sizes["ctx"] == 2 and sizes["pipe"] == 4
    return jax.shard_map(
        shards_line if on_line else shards_any,
        mesh=mesh,
        in_specs=(
            P(("pipe", "ctx"), "tp", None),
            P(("pipe", "ctx"), "tp", None),
            P(("pipe", "ctx"), "tp", None),
            P(("pipe", "ctx")),
            P("tp", "ctx"),
        ),
        out_specs=P("pipe", None, "tp", None, "ctx"),
        check_vma=False,
    )
```

```python
import functools

import jax
import jax.numpy as jnp
from jax import lax
from jax.experimental import pallas as pl
from jax.experimental.pallas import tpu as pltpu
from jax.sharding import PartitionSpec as P

BF16 = jnp.bfloat16
F32 = jnp.float32
LOG2E = 1.4426950408889634
MIB = 1 << 20

WEIGHT_CUTS = 2
OUTER = ((0, 1), (1, 0), (2, 3), (3, 2))
INNER = tuple(
    (p * 8 + c * 4 + t, p * 8 + c * 4 + 3 - t if t in (1, 2) else (p ^ 1) * 8 + c * 4 + t)
    for p in range(4)
    for c in range(2)
    for t in range(4)
)


def pin(value):
    return pltpu.with_memory_space_constraint(value, pltpu.HBM)


def pack_kernel(key_ref, value_ref, doc_ref, out_ref, marks, sems):
    rows = key_ref.shape[0]
    copies = [
        pltpu.make_async_copy(doc_ref, marks, sems.at[0]),
        pltpu.make_async_copy(key_ref, out_ref.at[pl.ds(0, rows)], sems.at[1]),
        pltpu.make_async_copy(value_ref, out_ref.at[pl.ds(rows, rows)], sems.at[2]),
    ]
    for copy in copies:
        copy.start()
    copies[0].wait()
    out_ref[2 * rows :] = jnp.broadcast_to(marks[...].astype(F32), (16, rows)).astype(BF16)
    copies[1].wait()
    copies[2].wait()


def pack(key_rows, value_rows, doc_ids):
    rows, _, width = key_rows.shape
    return pl.pallas_call(
        pack_kernel,
        out_shape=jax.ShapeDtypeStruct((2 * rows + 16, width), BF16),
        in_specs=[pl.BlockSpec(memory_space=pltpu.HBM)] * 3,
        out_specs=pl.BlockSpec(memory_space=pltpu.VMEM),
        scratch_shapes=[pltpu.VMEM((1, rows), jnp.int32), pltpu.SemaphoreType.DMA((3,))],
        compiler_params=pltpu.CompilerParams(vmem_limit_bytes=24 * MIB),
    )(
        *(
            pin(value)
            for value in (
                key_rows.reshape(rows, width),
                value_rows.reshape(rows, width),
                doc_ids.reshape(1, rows),
            )
        )
    )


def leaving(line):
    upper = line < 2
    inside = (line == 1) | (line == 2)
    return (
        jnp.where(upper, 3, 0),
        jnp.where(upper, 2, 1),
        jnp.where(inside, jnp.where(upper, 0, 3), jnp.where(upper, 1, 2)),
        line,
    )


def attend(window, heads, shards, query_all, blocks, scratch, result):
    keys, values, marks, own, bias = scratch
    rows, width = blocks[0].shape[0] // 2 - 8, blocks[0].shape[1]
    quarter = rows // 4
    half = 2 * quarter
    mine = lax.axis_index(("pipe", "ctx"))

    for s in range(window - 1):

        @pl.when(mine + s < window - 1)
        def _(s=s):
            at = slice(s * rows, (s + 1) * rows)
            keys[at] = jnp.zeros((rows, width), BF16)
            values[at, :] = jnp.zeros((rows, width), BF16)
            marks[s] = jnp.full((8, rows), -1.0, F32)

    for m in range(8):
        slot = (mine ^ m) - mine + window - 1

        @pl.when((slot >= 0) & (slot < window))
        def _(m=m, slot=slot):
            at = pl.ds(pl.multiple_of(slot * rows, rows), rows)
            keys[at, :] = blocks[m][:rows]
            values[at, :] = blocks[m][rows : 2 * rows]
            marks[slot] = blocks[m][2 * rows :].astype(F32)[:8]

    own[...] = jnp.transpose(jnp.broadcast_to(marks[window - 1][:1], (rows, rows)))
    for i, shard in enumerate(shards):
        start = pl.multiple_of(shard * quarter, quarter)
        here = own[pl.ds(start, quarter), :]
        for s in range(window):
            allowed = here == marks[s][:1]
            if s == window - 1:
                at_row = lax.broadcasted_iota(jnp.int32, (quarter, rows), 0) + start
                at_col = lax.broadcasted_iota(jnp.int32, (quarter, rows), 1)
                allowed = allowed & (at_col <= at_row)
            bias[i * quarter : (i + 1) * quarter, s * rows : (s + 1) * rows] = jnp.where(
                allowed, 0.0, -1e30
            )

    factor = LOG2E * width**-0.5
    group = 8
    for g in range(heads // group):
        query = query_all[g * group * half : (g + 1) * group * half]
        scores = lax.dot_general(
            query, keys[...], (((1,), (1,)), ((), ())), preferred_element_type=F32
        )
        parts, totals = [], []
        for j in range(group):
            shifted = scores[j * half : (j + 1) * half] + bias[...]
            peak = jnp.max(shifted, axis=1, keepdims=True)
            weights = jnp.exp2((shifted - peak) * factor)
            totals.append(jnp.sum(weights, axis=1, keepdims=True))
            parts.append(weights.astype(BF16))
        summed = jnp.dot(
            jnp.concatenate(parts, axis=0), values[...], preferred_element_type=F32
        )
        for j in range(group):
            h = g * group + j
            done = (summed[j * half : (j + 1) * half] / totals[j]).astype(BF16)
            result[:, h * width : (h + 1) * width] = done


def project(rows, weight, outs, left):
    tile = 1024 if weight.shape[1] % 1024 == 0 else weight.shape[1]
    for i in range(weight.shape[1] // tile):
        part = weight[:, i * tile : (i + 1) * tile]
        product = jnp.dot(rows, part, preferred_element_type=F32).astype(BF16)
        at, top = slice(left + i * tile, left + (i + 1) * tile), 0
        for out in outs:
            out[:, at] = product[top : top + out.shape[0]]
            top += out.shape[0]


def filled(rows):
    return jnp.concatenate([rows, jnp.zeros_like(rows)], axis=0)


def far_kernel(window, heads, query_ref, loaded_ref, weight_ref, *refs):
    blocks, (rows_out, early, part_ref) = refs[:8], refs[8:11]
    scratch, sems = refs[11:-1], refs[-1]
    copies = pieces(weight_ref, part_ref, loaded_ref.shape[1], WEIGHT_CUTS, sems)
    for copy in copies:
        copy.start()
    shards = leaving(lax.axis_index("tp"))[:2]
    attend(window, heads, shards, query_ref, blocks, scratch, rows_out)
    project(filled(rows_out[...]), loaded_ref, (early,), 0)
    for copy in copies:
        copy.wait()


def rest_kernel(left, rows_ref, loaded_ref, weight_ref, early, part_ref, sems):
    copies = pieces(weight_ref, part_ref, left, WEIGHT_CUTS, sems)
    for copy in copies:
        copy.start()
    rows = filled(rows_ref[...])
    project(rows, loaded_ref, (early,), 0)
    for copy in copies:
        copy.wait()
    project(rows, part_ref, (early,), loaded_ref.shape[1])


def rest_call(rows, loaded, weight):
    (half, depth), columns = rows.shape, weight.shape[1]
    vmem = pl.BlockSpec(memory_space=pltpu.VMEM)
    width = columns // 4
    return pl.pallas_call(
        functools.partial(rest_kernel, columns - width),
        out_shape=[
            jax.ShapeDtypeStruct((half, 2 * width), BF16),
            pltpu.VMEM((depth, width), BF16),
        ],
        in_specs=[vmem, vmem, pl.BlockSpec(memory_space=pltpu.HBM)],
        out_specs=[vmem, vmem],
        scratch_shapes=[pltpu.SemaphoreType.DMA((WEIGHT_CUTS,))],
        compiler_params=pltpu.CompilerParams(vmem_limit_bytes=24 * MIB),
        cost_estimate=pl.CostEstimate(
            flops=2 * half * depth * columns // 2, bytes_accessed=depth * columns, transcendentals=0
        ),
    )(rows, loaded, pin(weight))


def near_kernel(window, heads, query_ref, *refs):
    shards = leaving(lax.axis_index("tp"))[2:]
    attend(window, heads, shards, query_ref, refs[:8], refs[9:], refs[8])


def attention_call(query, blocks, window, weight=None):
    width = query.shape[1]
    rows = blocks[0].shape[0] // 2 - 8
    half = rows // 2
    heads = query.shape[0] // half
    vmem = pl.BlockSpec(memory_space=pltpu.VMEM)
    scratch = [
        pltpu.VMEM((window * rows, width), BF16),
        pltpu.VMEM((window * rows, width), BF16),
        pltpu.VMEM((window, 8, rows), F32),
        pltpu.VMEM((rows, rows), F32),
        pltpu.VMEM((half, window * rows), F32),
    ]
    flops = 4 * half * heads * window * rows * width
    outs = [jax.ShapeDtypeStruct((half, heads * width), BF16)]
    given, specs = [query], [vmem]
    kernel = near_kernel
    if weight is not None:
        (depth, columns), loaded = weight[1].shape, weight[0].shape[1]
        outs.append(jax.ShapeDtypeStruct((half, loaded), BF16))
        outs.append(pltpu.VMEM((depth, columns // 4), BF16))
        given += [weight[0], pin(weight[1])]
        specs += [vmem, pl.BlockSpec(memory_space=pltpu.HBM)]
        scratch.append(pltpu.SemaphoreType.DMA((WEIGHT_CUTS,)))
        flops += 2 * half * depth * loaded
        kernel = far_kernel
    return pl.pallas_call(
        functools.partial(kernel, window, heads),
        out_shape=outs,
        in_specs=specs + [vmem] * 8,
        out_specs=[vmem] * len(outs),
        scratch_shapes=scratch,
        compiler_params=pltpu.CompilerParams(vmem_limit_bytes=24 * MIB),
        cost_estimate=pl.CostEstimate(
            flops=flops, bytes_accessed=MIB, transcendentals=half * heads * window * rows
        ),
    )(*given, *blocks)


def project_kernel(count, *refs):
    rows = [ref[...] for ref in refs[:count]]
    rows = filled(rows[0]) if count == 1 else jnp.concatenate(rows, axis=0)
    left = 0
    for weight in refs[count : count + 3]:
        project(rows, weight, refs[count + 3 :], left)
        left += weight.shape[1]


def project_call(parts, weights):
    depth = parts[0].shape[1]
    columns = sum(weight.shape[1] for weight in weights)
    half = parts[0].shape[0]
    vmem = pl.BlockSpec(memory_space=pltpu.VMEM)
    outs = [jax.ShapeDtypeStruct((half // 2, columns), BF16)] * (2 * len(parts))
    return pl.pallas_call(
        functools.partial(project_kernel, len(parts)),
        out_shape=outs,
        in_specs=[vmem] * (len(parts) + 3),
        out_specs=[vmem] * len(outs),
        compiler_params=pltpu.CompilerParams(vmem_limit_bytes=24 * MIB),
        cost_estimate=pl.CostEstimate(
            flops=2 * half * len(parts) * depth * columns,
            bytes_accessed=2 * depth * columns,
            transcendentals=0,
        ),
    )(*parts, *weights)


def pieces(weight_ref, part_ref, left, count, sems):
    depth, columns = part_ref.shape
    rows = depth // count
    return [
        pltpu.make_async_copy(
            weight_ref.at[pl.ds(i * rows, rows), pl.ds(left, columns)],
            part_ref.at[pl.ds(i * rows, rows)],
            sems.at[i],
        )
        for i in range(count)
    ]


def load_kernel(heads, weight_ref, query_ref, out_ref, far_ref, near_ref, query_in, wide, sems):
    size = query_ref.shape[0] // 4
    half = 2 * size // heads
    copies = [
        pltpu.make_async_copy(
            query_ref.at[pl.ds(pl.multiple_of(shard * size, size), size)],
            query_in.at[pl.ds(i * size, size)],
            sems.at[i],
        )
        for i, shard in enumerate(leaving(lax.axis_index("tp")))
    ]
    copies += pieces(weight_ref, out_ref, 0, WEIGHT_CUTS, sems.at[pl.ds(4, WEIGHT_CUTS)])
    for copy in copies:
        copy.start()
    for copy in copies[:4]:
        copy.wait()
    wide[...] = query_in[...].astype(F32)
    for part, ref in enumerate((far_ref, near_ref)):
        for h in range(heads):
            start = part * half * heads + h
            ref[h * half : (h + 1) * half] = wide[pl.ds(start, half, stride=heads), :].astype(BF16)
    for copy in copies[4:]:
        copy.wait()


def load(weight, query):
    rows, heads, width = query.shape
    depth, columns = weight.shape
    hbm, vmem = pl.BlockSpec(memory_space=pltpu.HBM), pl.BlockSpec(memory_space=pltpu.VMEM)
    part = pltpu.VMEM((rows // 2 * heads, width), BF16)
    return pl.pallas_call(
        functools.partial(load_kernel, heads),
        out_shape=[pltpu.VMEM((depth, columns // 2), BF16), part, part],
        in_specs=[hbm, hbm],
        out_specs=[vmem] * 3,
        scratch_shapes=[
            pltpu.VMEM((rows * heads, width), BF16),
            pltpu.VMEM((rows * heads, width), F32),
            pltpu.SemaphoreType.DMA((4 + WEIGHT_CUTS,)),
        ],
        compiler_params=pltpu.CompilerParams(vmem_limit_bytes=24 * MIB),
        cost_estimate=pl.CostEstimate(flops=0, bytes_accessed=weight.size * 4, transcendentals=0),
    )(pin(weight), pin(query.reshape(rows * heads, width)))


def swap(value):
    return lax.ppermute(value, "tp", OUTER)


def send(value):
    return lax.ppermute(value, "tp", ((0, 1), (3, 2)))


def swap_inner(value):
    return lax.ppermute(value, ("pipe", "ctx", "tp"), INNER)


def shards_line(query_rows, key_rows, value_rows, doc_ids, out_weight):
    rows, heads, width = query_rows.shape
    columns = out_weight.shape[1]
    window = (lax.axis_size("pipe") * lax.axis_size("ctx")) // 2 + 1
    packed = pack(key_rows, value_rows, doc_ids)

    def pair(value, m):
        return lax.ppermute(value, ("pipe", "ctx"), [(i, i ^ m) for i in range(8)])

    by_x, by_y, by_both = pair(packed, 4), pair(packed, 1), pair(packed, 5)
    by_core = pair(packed, 2)
    after = lax.optimization_barrier
    line = lax.axis_index("tp")
    weight_here, inside = after((out_weight, (line == 1) | (line == 2)))
    weight, far_query, near_query = load(weight_here, query_rows)
    by_both, weight = after((by_both, weight))
    by_x, weight = after((by_x, weight))
    by_y, weight = after((by_y, weight))
    blocks = [packed, by_y, by_core, pair(by_y, 2), by_x, by_both, pair(by_x, 2), pair(by_both, 2)]

    def trade(value):
        return lax.ppermute(value, "ctx", [(0, 1), (1, 0)])

    def passed(value):
        return jnp.where(inside, value, jnp.zeros_like(value))

    far_rows, early, part = attention_call(far_query, blocks, window, (weight, out_weight))
    early_rest, last = rest_call(far_rows, part, out_weight)
    weights = (weight, part, last)
    early_in = swap(early)
    other_far = trade(far_rows)
    passed_on = swap_inner(early + early_in)
    rest_in = swap(early_rest)
    late_first, late_second = project_call([other_far], weights)
    first_in = swap(late_first)
    second_in = send(late_second)
    passed_rest = swap_inner(early_rest + rest_in)
    late_near = swap_inner(late_second + second_in)
    near_query, _ = after((near_query, early_rest))
    quarter = rows // 4
    both = passed(jnp.concatenate([passed_on, passed_rest], axis=1))
    (near_rows,) = attention_call(near_query, blocks, window)
    other_near = trade(near_rows)
    other_near, _ = after((other_near, passed_on))
    third, kept, late_third, late_kept = project_call([near_rows, other_near], weights)
    first_in, _ = after((first_in, third))
    late_far = swap_inner(late_first + first_in)
    last_in = swap(late_third + passed(late_far))
    other = late_kept + last_in + passed(late_near)
    third_in = swap(third + both[:quarter])
    third_in, _ = after((third_in, last_in))
    own = kept + third_in + both[quarter:]
    at_first = lax.axis_index("ctx") == 0
    both = jnp.stack([jnp.where(at_first, own, other), jnp.where(at_first, other, own)])
    return both.reshape(1, 2, 1, rows // 4, columns)


def shards_any(query_rows, key_rows, value_rows, doc_ids, out_weight):
    rows, heads, width = query_rows.shape
    kv_local = key_rows.shape[1]
    group = heads // kv_local
    mine = lax.axis_index(("pipe", "ctx"))
    marks = doc_ids.astype(BF16)
    keys = lax.all_gather(key_rows, ("pipe", "ctx"), axis=0, tiled=True)
    values = lax.all_gather(value_rows, ("pipe", "ctx"), axis=0, tiled=True)
    key_doc = lax.all_gather(marks, ("pipe", "ctx"), axis=0, tiled=True).astype(jnp.int32)
    key_pos = jnp.arange(keys.shape[0], dtype=jnp.int32)
    half = rows // 2
    done = []
    for part in range(2):
        at = slice(part * half, (part + 1) * half)
        query = query_rows[at].reshape(half, kv_local, group, width)
        query_pos = mine * rows + part * half + jnp.arange(half, dtype=jnp.int32)
        scores = jnp.einsum("qjgd,kjd->qjgk", query, keys, preferred_element_type=F32)
        scores = scores * width**-0.5
        allowed = (key_pos[None, :] <= query_pos[:, None]) & (
            key_doc[None, :] == doc_ids[at][:, None]
        )
        allowed = allowed[:, None, None, :]
        masked = jnp.where(allowed, scores, -1e30)
        peak = jnp.max(masked, axis=3, keepdims=True)
        weights = jnp.where(allowed, jnp.exp(scores - peak), 0.0)
        total = jnp.sum(weights, axis=3)
        summed = jnp.einsum(
            "qjgk,kjd->qjgd", weights.astype(BF16), values, preferred_element_type=F32
        )
        done.append((summed / total[..., None]).astype(BF16).reshape(half, heads * width))
    flat = jnp.concatenate(done, axis=0)
    tp_size, ctx_size = lax.axis_size("tp"), lax.axis_size("ctx")
    quarter, columns = rows // tp_size, out_weight.shape[1]
    partial = jnp.dot(
        lax.all_gather(flat, "ctx", axis=0, tiled=True), out_weight, preferred_element_type=F32
    )
    partial = partial.reshape(ctx_size, tp_size, quarter, columns)
    summed = lax.psum_scatter(partial.astype(BF16), "tp", scatter_dimension=1, tiled=True)
    return summed.reshape(1, ctx_size, 1, quarter, columns)


def solution(mesh):
    sizes = dict(mesh.shape)
    on_line = sizes["tp"] == 4 and sizes["ctx"] == 2 and sizes["pipe"] == 4
    return jax.shard_map(
        shards_line if on_line else shards_any,
        mesh=mesh,
        in_specs=(
            P(("pipe", "ctx"), "tp", None),
            P(("pipe", "ctx"), "tp", None),
            P(("pipe", "ctx"), "tp", None),
            P(("pipe", "ctx")),
            P("tp", "ctx"),
        ),
        out_specs=P("pipe", None, "tp", None, "ctx"),
        check_vma=False,
    )
```

```python
import functools

import jax
import jax.numpy as jnp
from jax import lax
from jax.experimental import pallas as pl
from jax.experimental.pallas import tpu as pltpu
from jax.sharding import PartitionSpec as P

BF16 = jnp.bfloat16
F32 = jnp.float32
LOG2E = 1.4426950408889634
MIB = 1 << 20

WEIGHT_CUTS = 1
OUTER = ((0, 1), (1, 0), (2, 3), (3, 2))
INNER = tuple(
    (p * 8 + c * 4 + t, p * 8 + c * 4 + 3 - t if t in (1, 2) else (p ^ 1) * 8 + c * 4 + t)
    for p in range(4)
    for c in range(2)
    for t in range(4)
)


def pin(value):
    return pltpu.with_memory_space_constraint(value, pltpu.HBM)


def pack_kernel(key_ref, value_ref, doc_ref, out_ref, marks, sems):
    rows = key_ref.shape[0]
    copies = [
        pltpu.make_async_copy(doc_ref, marks, sems.at[0]),
        pltpu.make_async_copy(key_ref, out_ref.at[pl.ds(0, rows)], sems.at[1]),
        pltpu.make_async_copy(value_ref, out_ref.at[pl.ds(rows, rows)], sems.at[2]),
    ]
    for copy in copies:
        copy.start()
    copies[0].wait()
    out_ref[2 * rows :] = jnp.broadcast_to(marks[...].astype(F32), (16, rows)).astype(BF16)
    copies[1].wait()
    copies[2].wait()


def pack(key_rows, value_rows, doc_ids):
    rows, _, width = key_rows.shape
    return pl.pallas_call(
        pack_kernel,
        out_shape=jax.ShapeDtypeStruct((2 * rows + 16, width), BF16),
        in_specs=[pl.BlockSpec(memory_space=pltpu.HBM)] * 3,
        out_specs=pl.BlockSpec(memory_space=pltpu.VMEM),
        scratch_shapes=[pltpu.VMEM((1, rows), jnp.int32), pltpu.SemaphoreType.DMA((3,))],
        compiler_params=pltpu.CompilerParams(vmem_limit_bytes=24 * MIB),
    )(
        *(
            pin(value)
            for value in (
                key_rows.reshape(rows, width),
                value_rows.reshape(rows, width),
                doc_ids.reshape(1, rows),
            )
        )
    )


def leaving(line):
    upper = line < 2
    inside = (line == 1) | (line == 2)
    return (
        jnp.where(upper, 3, 0),
        jnp.where(upper, 2, 1),
        jnp.where(inside, jnp.where(upper, 0, 3), jnp.where(upper, 1, 2)),
        line,
    )


def attend(window, heads, shards, query_all, blocks, scratch, result):
    keys, values, marks, own, bias = scratch
    rows, width = blocks[0].shape[0] // 2 - 8, blocks[0].shape[1]
    quarter = rows // 4
    half = 2 * quarter
    mine = lax.axis_index(("pipe", "ctx"))

    for s in range(window - 1):

        @pl.when(mine + s < window - 1)
        def _(s=s):
            at = slice(s * rows, (s + 1) * rows)
            keys[at] = jnp.zeros((rows, width), BF16)
            values[at, :] = jnp.zeros((rows, width), BF16)
            marks[s] = jnp.full((8, rows), -1.0, F32)

    for m in range(8):
        slot = (mine ^ m) - mine + window - 1

        @pl.when((slot >= 0) & (slot < window))
        def _(m=m, slot=slot):
            at = pl.ds(pl.multiple_of(slot * rows, rows), rows)
            keys[at, :] = blocks[m][:rows]
            values[at, :] = blocks[m][rows : 2 * rows]
            marks[slot] = blocks[m][2 * rows :].astype(F32)[:8]

    own[...] = jnp.transpose(jnp.broadcast_to(marks[window - 1][:1], (rows, rows)))
    for i, shard in enumerate(shards):
        start = pl.multiple_of(shard * quarter, quarter)
        here = own[pl.ds(start, quarter), :]
        for s in range(window):
            allowed = here == marks[s][:1]
            if s == window - 1:
                at_row = lax.broadcasted_iota(jnp.int32, (quarter, rows), 0) + start
                at_col = lax.broadcasted_iota(jnp.int32, (quarter, rows), 1)
                allowed = allowed & (at_col <= at_row)
            bias[i * quarter : (i + 1) * quarter, s * rows : (s + 1) * rows] = jnp.where(
                allowed, 0.0, -1e30
            )

    factor = LOG2E * width**-0.5
    group = 8
    for g in range(heads // group):
        query = query_all[g * group * half : (g + 1) * group * half]
        scores = lax.dot_general(
            query, keys[...], (((1,), (1,)), ((), ())), preferred_element_type=F32
        )
        parts, totals = [], []
        for j in range(group):
            shifted = scores[j * half : (j + 1) * half] + bias[...]
            peak = jnp.max(shifted, axis=1, keepdims=True)
            weights = jnp.exp2((shifted - peak) * factor)
            totals.append(jnp.sum(weights, axis=1, keepdims=True))
            parts.append(weights.astype(BF16))
        summed = jnp.dot(
            jnp.concatenate(parts, axis=0), values[...], preferred_element_type=F32
        )
        for j in range(group):
            h = g * group + j
            done = (summed[j * half : (j + 1) * half] / totals[j]).astype(BF16)
            result[:, h * width : (h + 1) * width] = done


def project(rows, weight, outs, left):
    tile = 1024 if weight.shape[1] % 1024 == 0 else weight.shape[1]
    for i in range(weight.shape[1] // tile):
        part = weight[:, i * tile : (i + 1) * tile]
        product = jnp.dot(rows, part, preferred_element_type=F32).astype(BF16)
        at, top = slice(left + i * tile, left + (i + 1) * tile), 0
        for out in outs:
            out[:, at] = product[top : top + out.shape[0]]
            top += out.shape[0]


def filled(rows):
    return jnp.concatenate([rows, jnp.zeros_like(rows)], axis=0)


def far_kernel(window, heads, query_ref, loaded_ref, weight_ref, *refs):
    blocks, (rows_out, early, part_ref) = refs[:8], refs[8:11]
    scratch, sems = refs[11:-1], refs[-1]
    copies = pieces(weight_ref, part_ref, loaded_ref.shape[1], WEIGHT_CUTS, sems)
    for copy in copies:
        copy.start()
    shards = leaving(lax.axis_index("tp"))[:2]
    attend(window, heads, shards, query_ref, blocks, scratch, rows_out)
    project(filled(rows_out[...]), loaded_ref, (early,), 0)
    for copy in copies:
        copy.wait()


def rest_kernel(left, rows_ref, loaded_ref, weight_ref, early, part_ref, sems):
    copies = pieces(weight_ref, part_ref, left, WEIGHT_CUTS, sems)
    for copy in copies:
        copy.start()
    rows = filled(rows_ref[...])
    project(rows, loaded_ref, (early,), 0)
    for copy in copies:
        copy.wait()
    project(rows, part_ref, (early,), loaded_ref.shape[1])


def rest_call(rows, loaded, weight):
    (half, depth), columns = rows.shape, weight.shape[1]
    vmem = pl.BlockSpec(memory_space=pltpu.VMEM)
    width = columns // 4
    return pl.pallas_call(
        functools.partial(rest_kernel, columns - width),
        out_shape=[
            jax.ShapeDtypeStruct((half, 2 * width), BF16),
            pltpu.VMEM((depth, width), BF16),
        ],
        in_specs=[vmem, vmem, pl.BlockSpec(memory_space=pltpu.HBM)],
        out_specs=[vmem, vmem],
        scratch_shapes=[pltpu.SemaphoreType.DMA((WEIGHT_CUTS,))],
        compiler_params=pltpu.CompilerParams(vmem_limit_bytes=24 * MIB),
        cost_estimate=pl.CostEstimate(
            flops=2 * half * depth * columns // 2, bytes_accessed=depth * columns, transcendentals=0
        ),
    )(rows, loaded, pin(weight))


def near_kernel(window, heads, query_ref, *refs):
    shards = leaving(lax.axis_index("tp"))[2:]
    attend(window, heads, shards, query_ref, refs[:8], refs[9:], refs[8])


def attention_call(query, blocks, window, weight=None):
    width = query.shape[1]
    rows = blocks[0].shape[0] // 2 - 8
    half = rows // 2
    heads = query.shape[0] // half
    vmem = pl.BlockSpec(memory_space=pltpu.VMEM)
    scratch = [
        pltpu.VMEM((window * rows, width), BF16),
        pltpu.VMEM((window * rows, width), BF16),
        pltpu.VMEM((window, 8, rows), F32),
        pltpu.VMEM((rows, rows), F32),
        pltpu.VMEM((half, window * rows), F32),
    ]
    flops = 4 * half * heads * window * rows * width
    outs = [jax.ShapeDtypeStruct((half, heads * width), BF16)]
    given, specs = [query], [vmem]
    kernel = near_kernel
    if weight is not None:
        (depth, columns), loaded = weight[1].shape, weight[0].shape[1]
        outs.append(jax.ShapeDtypeStruct((half, loaded), BF16))
        outs.append(pltpu.VMEM((depth, columns // 4), BF16))
        given += [weight[0], pin(weight[1])]
        specs += [vmem, pl.BlockSpec(memory_space=pltpu.HBM)]
        scratch.append(pltpu.SemaphoreType.DMA((WEIGHT_CUTS,)))
        flops += 2 * half * depth * loaded
        kernel = far_kernel
    return pl.pallas_call(
        functools.partial(kernel, window, heads),
        out_shape=outs,
        in_specs=specs + [vmem] * 8,
        out_specs=[vmem] * len(outs),
        scratch_shapes=scratch,
        compiler_params=pltpu.CompilerParams(vmem_limit_bytes=24 * MIB),
        cost_estimate=pl.CostEstimate(
            flops=flops, bytes_accessed=MIB, transcendentals=half * heads * window * rows
        ),
    )(*given, *blocks)


def project_kernel(count, *refs):
    rows = [ref[...] for ref in refs[:count]]
    rows = filled(rows[0]) if count == 1 else jnp.concatenate(rows, axis=0)
    left = 0
    for weight in refs[count : count + 3]:
        project(rows, weight, refs[count + 3 :], left)
        left += weight.shape[1]


def project_call(parts, weights):
    depth = parts[0].shape[1]
    columns = sum(weight.shape[1] for weight in weights)
    half = parts[0].shape[0]
    vmem = pl.BlockSpec(memory_space=pltpu.VMEM)
    outs = [jax.ShapeDtypeStruct((half // 2, columns), BF16)] * (2 * len(parts))
    return pl.pallas_call(
        functools.partial(project_kernel, len(parts)),
        out_shape=outs,
        in_specs=[vmem] * (len(parts) + 3),
        out_specs=[vmem] * len(outs),
        compiler_params=pltpu.CompilerParams(vmem_limit_bytes=24 * MIB),
        cost_estimate=pl.CostEstimate(
            flops=2 * half * len(parts) * depth * columns,
            bytes_accessed=2 * depth * columns,
            transcendentals=0,
        ),
    )(*parts, *weights)


def pieces(weight_ref, part_ref, left, count, sems):
    depth, columns = part_ref.shape
    rows = depth // count
    return [
        pltpu.make_async_copy(
            weight_ref.at[pl.ds(i * rows, rows), pl.ds(left, columns)],
            part_ref.at[pl.ds(i * rows, rows)],
            sems.at[i],
        )
        for i in range(count)
    ]


def load_kernel(heads, weight_ref, query_ref, out_ref, far_ref, near_ref, query_in, wide, sems):
    size = query_ref.shape[0] // 4
    half = 2 * size // heads
    copies = [
        pltpu.make_async_copy(
            query_ref.at[pl.ds(pl.multiple_of(shard * size, size), size)],
            query_in.at[pl.ds(i * size, size)],
            sems.at[i],
        )
        for i, shard in enumerate(leaving(lax.axis_index("tp")))
    ]
    copies += pieces(weight_ref, out_ref, 0, WEIGHT_CUTS, sems.at[pl.ds(4, WEIGHT_CUTS)])
    for copy in copies:
        copy.start()
    for copy in copies[:4]:
        copy.wait()
    wide[: query_in.shape[0]] = query_in[...].astype(F32)
    for part, ref in enumerate((far_ref, near_ref)):
        for h in range(heads):
            start = part * half * heads + h
            ref[h * half : (h + 1) * half] = wide[pl.ds(start, half, stride=heads), :].astype(BF16)
    for copy in copies[4:]:
        copy.wait()


def load(weight, query):
    rows, heads, width = query.shape
    depth, columns = weight.shape
    hbm, vmem = pl.BlockSpec(memory_space=pltpu.HBM), pl.BlockSpec(memory_space=pltpu.VMEM)
    part = pltpu.VMEM((rows // 2 * heads, width), BF16)
    return pl.pallas_call(
        functools.partial(load_kernel, heads),
        out_shape=[pltpu.VMEM((depth, columns // 2), BF16), part, part],
        in_specs=[hbm, hbm],
        out_specs=[vmem] * 3,
        scratch_shapes=[
            pltpu.VMEM((rows * heads, width), BF16),
            pltpu.VMEM((rows * heads + heads, width), F32),
            pltpu.SemaphoreType.DMA((4 + WEIGHT_CUTS,)),
        ],
        compiler_params=pltpu.CompilerParams(vmem_limit_bytes=24 * MIB),
        cost_estimate=pl.CostEstimate(flops=0, bytes_accessed=weight.size * 4, transcendentals=0),
    )(pin(weight), pin(query.reshape(rows * heads, width)))


def swap(value):
    return lax.ppermute(value, "tp", OUTER)


def send(value):
    return lax.ppermute(value, "tp", ((0, 1), (3, 2)))


def swap_inner(value):
    return lax.ppermute(value, ("pipe", "ctx", "tp"), INNER)


def shards_line(query_rows, key_rows, value_rows, doc_ids, out_weight):
    rows, heads, width = query_rows.shape
    columns = out_weight.shape[1]
    window = (lax.axis_size("pipe") * lax.axis_size("ctx")) // 2 + 1
    packed = pack(key_rows, value_rows, doc_ids)

    def pair(value, m):
        return lax.ppermute(value, ("pipe", "ctx"), [(i, i ^ m) for i in range(8)])

    by_x, by_y, by_both = pair(packed, 4), pair(packed, 1), pair(packed, 5)
    by_core = pair(packed, 2)
    after = lax.optimization_barrier
    line = lax.axis_index("tp")
    weight_here, inside = after((out_weight, (line == 1) | (line == 2)))
    weight, far_query, near_query = load(weight_here, query_rows)
    by_both, weight = after((by_both, weight))
    by_x, weight = after((by_x, weight))
    by_y, weight = after((by_y, weight))
    blocks = [packed, by_y, by_core, pair(by_y, 2), by_x, by_both, pair(by_x, 2), pair(by_both, 2)]

    def trade(value):
        return lax.ppermute(value, "ctx", [(0, 1), (1, 0)])

    def passed(value):
        return jnp.where(inside, value, jnp.zeros_like(value))

    far_rows, early, part = attention_call(far_query, blocks, window, (weight, out_weight))
    early_rest, last = rest_call(far_rows, part, out_weight)
    weights = (weight, part, last)
    early_in = swap(early)
    other_far = trade(far_rows)
    passed_on = swap_inner(early + early_in)
    rest_in = swap(early_rest)
    late_first, late_second = project_call([other_far], weights)
    first_in = swap(late_first)
    second_in = send(late_second)
    passed_rest = swap_inner(early_rest + rest_in)
    late_near = swap_inner(late_second + second_in)
    near_query, _ = after((near_query, early_rest))
    quarter = rows // 4
    both = passed(jnp.concatenate([passed_on, passed_rest], axis=1))
    (near_rows,) = attention_call(near_query, blocks, window)
    other_near = trade(near_rows)
    other_near, _ = after((other_near, passed_on))
    third, kept, late_third, late_kept = project_call([near_rows, other_near], weights)
    first_in, _ = after((first_in, third))
    late_far = swap_inner(late_first + first_in)
    last_in = swap(late_third + passed(late_far))
    other = late_kept + last_in + passed(late_near)
    third_in = swap(third + both[:quarter])
    third_in, _ = after((third_in, last_in))
    own = kept + third_in + both[quarter:]
    at_first = lax.axis_index("ctx") == 0
    both = jnp.stack([jnp.where(at_first, own, other), jnp.where(at_first, other, own)])
    return both.reshape(1, 2, 1, rows // 4, columns)


def shards_any(query_rows, key_rows, value_rows, doc_ids, out_weight):
    rows, heads, width = query_rows.shape
    kv_local = key_rows.shape[1]
    group = heads // kv_local
    mine = lax.axis_index(("pipe", "ctx"))
    marks = doc_ids.astype(BF16)
    keys = lax.all_gather(key_rows, ("pipe", "ctx"), axis=0, tiled=True)
    values = lax.all_gather(value_rows, ("pipe", "ctx"), axis=0, tiled=True)
    key_doc = lax.all_gather(marks, ("pipe", "ctx"), axis=0, tiled=True).astype(jnp.int32)
    key_pos = jnp.arange(keys.shape[0], dtype=jnp.int32)
    half = rows // 2
    done = []
    for part in range(2):
        at = slice(part * half, (part + 1) * half)
        query = query_rows[at].reshape(half, kv_local, group, width)
        query_pos = mine * rows + part * half + jnp.arange(half, dtype=jnp.int32)
        scores = jnp.einsum("qjgd,kjd->qjgk", query, keys, preferred_element_type=F32)
        scores = scores * width**-0.5
        allowed = (key_pos[None, :] <= query_pos[:, None]) & (
            key_doc[None, :] == doc_ids[at][:, None]
        )
        allowed = allowed[:, None, None, :]
        masked = jnp.where(allowed, scores, -1e30)
        peak = jnp.max(masked, axis=3, keepdims=True)
        weights = jnp.where(allowed, jnp.exp(scores - peak), 0.0)
        total = jnp.sum(weights, axis=3)
        summed = jnp.einsum(
            "qjgk,kjd->qjgd", weights.astype(BF16), values, preferred_element_type=F32
        )
        done.append((summed / total[..., None]).astype(BF16).reshape(half, heads * width))
    flat = jnp.concatenate(done, axis=0)
    tp_size, ctx_size = lax.axis_size("tp"), lax.axis_size("ctx")
    quarter, columns = rows // tp_size, out_weight.shape[1]
    partial = jnp.dot(
        lax.all_gather(flat, "ctx", axis=0, tiled=True), out_weight, preferred_element_type=F32
    )
    partial = partial.reshape(ctx_size, tp_size, quarter, columns)
    summed = lax.psum_scatter(partial.astype(BF16), "tp", scatter_dimension=1, tiled=True)
    return summed.reshape(1, ctx_size, 1, quarter, columns)


def solution(mesh):
    sizes = dict(mesh.shape)
    on_line = sizes["tp"] == 4 and sizes["ctx"] == 2 and sizes["pipe"] == 4
    return jax.shard_map(
        shards_line if on_line else shards_any,
        mesh=mesh,
        in_specs=(
            P(("pipe", "ctx"), "tp", None),
            P(("pipe", "ctx"), "tp", None),
            P(("pipe", "ctx"), "tp", None),
            P(("pipe", "ctx")),
            P("tp", "ctx"),
        ),
        out_specs=P("pipe", None, "tp", None, "ctx"),
        check_vma=False,
    )
```

```python
import functools

import jax
import jax.numpy as jnp
from jax import lax
from jax.experimental import pallas as pl
from jax.experimental.pallas import tpu as pltpu
from jax.sharding import PartitionSpec as P

BF16 = jnp.bfloat16
F32 = jnp.float32
LOG2E = 1.4426950408889634
MIB = 1 << 20

WEIGHT_CUTS = 1
OUTER = ((0, 1), (1, 0), (2, 3), (3, 2))
INNER = tuple(
    (p * 8 + c * 4 + t, p * 8 + c * 4 + 3 - t if t in (1, 2) else (p ^ 1) * 8 + c * 4 + t)
    for p in range(4)
    for c in range(2)
    for t in range(4)
)


def pin(value):
    return pltpu.with_memory_space_constraint(value, pltpu.HBM)


def pack_kernel(key_ref, value_ref, doc_ref, out_ref, marks, sems):
    rows = key_ref.shape[0]
    copies = [
        pltpu.make_async_copy(doc_ref, marks, sems.at[0]),
        pltpu.make_async_copy(key_ref, out_ref.at[pl.ds(0, rows)], sems.at[1]),
        pltpu.make_async_copy(value_ref, out_ref.at[pl.ds(rows, rows)], sems.at[2]),
    ]
    for copy in copies:
        copy.start()
    copies[0].wait()
    out_ref[2 * rows :] = jnp.broadcast_to(marks[...].astype(F32), (16, rows)).astype(BF16)
    copies[1].wait()
    copies[2].wait()


def pack(key_rows, value_rows, doc_ids):
    rows, _, width = key_rows.shape
    return pl.pallas_call(
        pack_kernel,
        out_shape=jax.ShapeDtypeStruct((2 * rows + 16, width), BF16),
        in_specs=[pl.BlockSpec(memory_space=pltpu.HBM)] * 3,
        out_specs=pl.BlockSpec(memory_space=pltpu.VMEM),
        scratch_shapes=[pltpu.VMEM((1, rows), jnp.int32), pltpu.SemaphoreType.DMA((3,))],
        compiler_params=pltpu.CompilerParams(vmem_limit_bytes=24 * MIB),
    )(
        *(
            pin(value)
            for value in (
                key_rows.reshape(rows, width),
                value_rows.reshape(rows, width),
                doc_ids.reshape(1, rows),
            )
        )
    )


def leaving(line):
    upper = line < 2
    inside = (line == 1) | (line == 2)
    return (
        jnp.where(upper, 3, 0),
        jnp.where(upper, 2, 1),
        jnp.where(inside, jnp.where(upper, 0, 3), jnp.where(upper, 1, 2)),
        line,
    )


def attend(window, heads, shards, query_all, blocks, scratch, result):
    keys, values, marks, own, bias = scratch
    rows, width = blocks[0].shape[0] // 2 - 8, blocks[0].shape[1]
    quarter = rows // 4
    half = 2 * quarter
    mine = lax.axis_index(("pipe", "ctx"))

    for s in range(window - 1):

        @pl.when(mine + s < window - 1)
        def _(s=s):
            at = slice(s * rows, (s + 1) * rows)
            keys[at] = jnp.zeros((rows, width), BF16)
            values[at, :] = jnp.zeros((rows, width), BF16)
            marks[s] = jnp.full((8, rows), -1.0, F32)

    for m in range(8):
        slot = (mine ^ m) - mine + window - 1

        @pl.when((slot >= 0) & (slot < window))
        def _(m=m, slot=slot):
            at = pl.ds(pl.multiple_of(slot * rows, rows), rows)
            keys[at, :] = blocks[m][:rows]
            values[at, :] = blocks[m][rows : 2 * rows]
            marks[slot] = blocks[m][2 * rows :].astype(F32)[:8]

    own[...] = jnp.transpose(jnp.broadcast_to(marks[window - 1][:1], (rows, rows)))
    for i, shard in enumerate(shards):
        start = pl.multiple_of(shard * quarter, quarter)
        here = own[pl.ds(start, quarter), :]
        for s in range(window):
            allowed = here == marks[s][:1]
            if s == window - 1:
                at_row = lax.broadcasted_iota(jnp.int32, (quarter, rows), 0) + start
                at_col = lax.broadcasted_iota(jnp.int32, (quarter, rows), 1)
                allowed = allowed & (at_col <= at_row)
            bias[i * quarter : (i + 1) * quarter, s * rows : (s + 1) * rows] = jnp.where(
                allowed, 0.0, -1e30
            )

    factor = LOG2E * width**-0.5
    group = 8
    for g in range(heads // group):
        query = query_all[g * group * half : (g + 1) * group * half]
        scores = lax.dot_general(
            query, keys[...], (((1,), (1,)), ((), ())), preferred_element_type=F32
        )
        parts, totals = [], []
        for j in range(group):
            shifted = scores[j * half : (j + 1) * half] + bias[...]
            peak = jnp.max(shifted, axis=1, keepdims=True)
            weights = jnp.exp2((shifted - peak) * factor)
            totals.append(jnp.sum(weights, axis=1, keepdims=True))
            parts.append(weights.astype(BF16))
        summed = jnp.dot(
            jnp.concatenate(parts, axis=0), values[...], preferred_element_type=F32
        )
        for j in range(group):
            h = g * group + j
            done = (summed[j * half : (j + 1) * half] / totals[j]).astype(BF16)
            result[:, h * width : (h + 1) * width] = done


def project(rows, weight, outs, left):
    tile = 1024 if weight.shape[1] % 1024 == 0 else weight.shape[1]
    for i in range(weight.shape[1] // tile):
        part = weight[:, i * tile : (i + 1) * tile]
        product = jnp.dot(rows, part, preferred_element_type=F32).astype(BF16)
        at, top = slice(left + i * tile, left + (i + 1) * tile), 0
        for out in outs:
            out[:, at] = product[top : top + out.shape[0]]
            top += out.shape[0]


def filled(rows):
    return jnp.concatenate([rows, jnp.zeros_like(rows)], axis=0)


def far_kernel(window, heads, query_ref, loaded_ref, weight_ref, *refs):
    blocks, (rows_out, early, part_ref) = refs[:8], refs[8:11]
    scratch, sems = refs[11:-1], refs[-1]
    copies = pieces(weight_ref, part_ref, loaded_ref.shape[1], WEIGHT_CUTS, sems)
    for copy in copies:
        copy.start()
    shards = leaving(lax.axis_index("tp"))[:2]
    attend(window, heads, shards, query_ref, blocks, scratch, rows_out)
    project(filled(rows_out[...]), loaded_ref, (early,), 0)
    for copy in copies:
        copy.wait()


def rest_kernel(left, rows_ref, loaded_ref, weight_ref, early, part_ref, sems):
    copies = pieces(weight_ref, part_ref, left, WEIGHT_CUTS, sems)
    for copy in copies:
        copy.start()
    rows = filled(rows_ref[...])
    project(rows, loaded_ref, (early,), 0)
    for copy in copies:
        copy.wait()
    project(rows, part_ref, (early,), loaded_ref.shape[1])


def rest_call(rows, loaded, weight):
    (half, depth), columns = rows.shape, weight.shape[1]
    vmem = pl.BlockSpec(memory_space=pltpu.VMEM)
    width = columns // 4
    return pl.pallas_call(
        functools.partial(rest_kernel, columns - width),
        out_shape=[
            jax.ShapeDtypeStruct((half, 2 * width), BF16),
            pltpu.VMEM((depth, width), BF16),
        ],
        in_specs=[vmem, vmem, pl.BlockSpec(memory_space=pltpu.HBM)],
        out_specs=[vmem, vmem],
        scratch_shapes=[pltpu.SemaphoreType.DMA((WEIGHT_CUTS,))],
        compiler_params=pltpu.CompilerParams(vmem_limit_bytes=24 * MIB),
        cost_estimate=pl.CostEstimate(
            flops=2 * half * depth * columns // 2, bytes_accessed=depth * columns, transcendentals=0
        ),
    )(rows, loaded, pin(weight))


def near_kernel(window, heads, query_ref, *refs):
    shards = leaving(lax.axis_index("tp"))[2:]
    attend(window, heads, shards, query_ref, refs[:8], refs[9:], refs[8])


def attention_call(query, blocks, window, weight=None):
    width = query.shape[1]
    rows = blocks[0].shape[0] // 2 - 8
    half = rows // 2
    heads = query.shape[0] // half
    vmem = pl.BlockSpec(memory_space=pltpu.VMEM)
    scratch = [
        pltpu.VMEM((window * rows, width), BF16),
        pltpu.VMEM((window * rows, width), BF16),
        pltpu.VMEM((window, 8, rows), F32),
        pltpu.VMEM((rows, rows), F32),
        pltpu.VMEM((half, window * rows), F32),
    ]
    flops = 4 * half * heads * window * rows * width
    outs = [jax.ShapeDtypeStruct((half, heads * width), BF16)]
    given, specs = [query], [vmem]
    kernel = near_kernel
    if weight is not None:
        (depth, columns), loaded = weight[1].shape, weight[0].shape[1]
        outs.append(jax.ShapeDtypeStruct((half, loaded), BF16))
        outs.append(pltpu.VMEM((depth, columns // 4), BF16))
        given += [weight[0], pin(weight[1])]
        specs += [vmem, pl.BlockSpec(memory_space=pltpu.HBM)]
        scratch.append(pltpu.SemaphoreType.DMA((WEIGHT_CUTS,)))
        flops += 2 * half * depth * loaded
        kernel = far_kernel
    return pl.pallas_call(
        functools.partial(kernel, window, heads),
        out_shape=outs,
        in_specs=specs + [vmem] * 8,
        out_specs=[vmem] * len(outs),
        scratch_shapes=scratch,
        compiler_params=pltpu.CompilerParams(vmem_limit_bytes=24 * MIB),
        cost_estimate=pl.CostEstimate(
            flops=flops, bytes_accessed=MIB, transcendentals=half * heads * window * rows
        ),
    )(*given, *blocks)


def project_kernel(count, *refs):
    rows = [ref[...] for ref in refs[:count]]
    rows = filled(rows[0]) if count == 1 else jnp.concatenate(rows, axis=0)
    left = 0
    for weight in refs[count : count + 3]:
        project(rows, weight, refs[count + 3 :], left)
        left += weight.shape[1]


def project_call(parts, weights):
    depth = parts[0].shape[1]
    columns = sum(weight.shape[1] for weight in weights)
    half = parts[0].shape[0]
    vmem = pl.BlockSpec(memory_space=pltpu.VMEM)
    outs = [jax.ShapeDtypeStruct((half // 2, columns), BF16)] * (2 * len(parts))
    return pl.pallas_call(
        functools.partial(project_kernel, len(parts)),
        out_shape=outs,
        in_specs=[vmem] * (len(parts) + 3),
        out_specs=[vmem] * len(outs),
        compiler_params=pltpu.CompilerParams(vmem_limit_bytes=24 * MIB),
        cost_estimate=pl.CostEstimate(
            flops=2 * half * len(parts) * depth * columns,
            bytes_accessed=2 * depth * columns,
            transcendentals=0,
        ),
    )(*parts, *weights)


def pieces(weight_ref, part_ref, left, count, sems):
    depth, columns = part_ref.shape
    rows = depth // count
    return [
        pltpu.make_async_copy(
            weight_ref.at[pl.ds(i * rows, rows), pl.ds(left, columns)],
            part_ref.at[pl.ds(i * rows, rows)],
            sems.at[i],
        )
        for i in range(count)
    ]


def load_kernel(heads, weight_ref, query_ref, out_ref, far_ref, near_ref, query_in, wide, sems):
    size = query_ref.shape[0] // 4
    half = 2 * size // heads
    copies = [
        pltpu.make_async_copy(
            query_ref.at[pl.ds(pl.multiple_of(shard * size, size), size)],
            query_in.at[pl.ds(i * size, size)],
            sems.at[i],
        )
        for i, shard in enumerate(leaving(lax.axis_index("tp")))
    ]
    copies += pieces(weight_ref, out_ref, 0, WEIGHT_CUTS, sems.at[pl.ds(4, WEIGHT_CUTS)])
    for copy in copies:
        copy.start()
    for copy in copies[:4]:
        copy.wait()
    wide[: query_in.shape[0]] = query_in[...].astype(F32)
    for part, ref in enumerate((far_ref, near_ref)):
        for h in range(heads):
            start = part * half * heads + h
            ref[h * half : (h + 1) * half] = wide[pl.ds(start, half, stride=heads), :].astype(BF16)
    for copy in copies[4:]:
        copy.wait()


def load(weight, query):
    rows, heads, width = query.shape
    depth, columns = weight.shape
    hbm, vmem = pl.BlockSpec(memory_space=pltpu.HBM), pl.BlockSpec(memory_space=pltpu.VMEM)
    part = pltpu.VMEM((rows // 2 * heads, width), BF16)
    return pl.pallas_call(
        functools.partial(load_kernel, heads),
        out_shape=[pltpu.VMEM((depth, columns // 2), BF16), part, part],
        in_specs=[hbm, hbm],
        out_specs=[vmem] * 3,
        scratch_shapes=[
            pltpu.VMEM((rows * heads, width), BF16),
            pltpu.VMEM((rows * heads + heads, width), F32),
            pltpu.SemaphoreType.DMA((4 + WEIGHT_CUTS,)),
        ],
        compiler_params=pltpu.CompilerParams(vmem_limit_bytes=24 * MIB),
        cost_estimate=pl.CostEstimate(flops=0, bytes_accessed=weight.size * 4, transcendentals=0),
    )(pin(weight), pin(query.reshape(rows * heads, width)))


def swap(value):
    return lax.ppermute(value, "tp", OUTER)


def send(value):
    return lax.ppermute(value, "tp", ((0, 1), (3, 2)))


def swap_inner(value):
    return lax.ppermute(value, ("pipe", "ctx", "tp"), INNER)


def shards_line(query_rows, key_rows, value_rows, doc_ids, out_weight):
    rows, heads, width = query_rows.shape
    columns = out_weight.shape[1]
    window = (lax.axis_size("pipe") * lax.axis_size("ctx")) // 2 + 1
    packed = pack(key_rows, value_rows, doc_ids)

    def pair(value, m):
        return lax.ppermute(value, ("pipe", "ctx"), [(i, i ^ m) for i in range(8)])

    by_x, by_y, by_both = pair(packed, 4), pair(packed, 1), pair(packed, 5)
    by_core = pair(packed, 2)
    after = lax.optimization_barrier
    line = lax.axis_index("tp")
    weight_here, inside = after((out_weight, (line == 1) | (line == 2)))
    weight, far_query, near_query = load(weight_here, query_rows)
    by_both, weight = after((by_both, weight))
    by_x, weight = after((by_x, weight))
    by_y, weight = after((by_y, weight))
    blocks = [packed, by_y, by_core, pair(by_y, 2), by_x, by_both, pair(by_x, 2), pair(by_both, 2)]

    def trade(value):
        return lax.ppermute(value, "ctx", [(0, 1), (1, 0)])

    def passed(value):
        return jnp.where(inside, value, jnp.zeros_like(value))

    far_rows, early, part = attention_call(far_query, blocks, window, (weight, out_weight))
    early_rest, last = rest_call(far_rows, part, out_weight)
    weights = (weight, part, last)
    early_in = swap(early)
    other_far = trade(far_rows)
    passed_on = swap_inner(early + early_in)
    rest_in = swap(early_rest)
    late_first, late_second = project_call([other_far], weights)
    first_in = swap(late_first)
    second_in = send(late_second)
    passed_rest = swap_inner(early_rest + rest_in)
    near_query, _ = after((near_query, early_rest))
    quarter = rows // 4
    both = passed(jnp.concatenate([passed_on, passed_rest], axis=1))
    (near_rows,) = attention_call(near_query, blocks, window)
    other_near = trade(near_rows)
    other_near, _ = after((other_near, passed_on))
    third, kept, late_third, late_kept = project_call([near_rows, other_near], weights)
    first_in, _ = after((first_in, third))
    second_in, _ = after((second_in, third))
    late_near = swap_inner(late_second + second_in)
    late_far = swap_inner(late_first + first_in)
    last_in = swap(late_third + passed(late_far))
    other = late_kept + last_in + passed(late_near)
    third_in = swap(third + both[:quarter])
    third_in, _ = after((third_in, last_in))
    own = kept + third_in + both[quarter:]
    at_first = lax.axis_index("ctx") == 0
    both = jnp.stack([jnp.where(at_first, own, other), jnp.where(at_first, other, own)])
    return both.reshape(1, 2, 1, rows // 4, columns)


def shards_any(query_rows, key_rows, value_rows, doc_ids, out_weight):
    rows, heads, width = query_rows.shape
    kv_local = key_rows.shape[1]
    group = heads // kv_local
    mine = lax.axis_index(("pipe", "ctx"))
    marks = doc_ids.astype(BF16)
    keys = lax.all_gather(key_rows, ("pipe", "ctx"), axis=0, tiled=True)
    values = lax.all_gather(value_rows, ("pipe", "ctx"), axis=0, tiled=True)
    key_doc = lax.all_gather(marks, ("pipe", "ctx"), axis=0, tiled=True).astype(jnp.int32)
    key_pos = jnp.arange(keys.shape[0], dtype=jnp.int32)
    half = rows // 2
    done = []
    for part in range(2):
        at = slice(part * half, (part + 1) * half)
        query = query_rows[at].reshape(half, kv_local, group, width)
        query_pos = mine * rows + part * half + jnp.arange(half, dtype=jnp.int32)
        scores = jnp.einsum("qjgd,kjd->qjgk", query, keys, preferred_element_type=F32)
        scores = scores * width**-0.5
        allowed = (key_pos[None, :] <= query_pos[:, None]) & (
            key_doc[None, :] == doc_ids[at][:, None]
        )
        allowed = allowed[:, None, None, :]
        masked = jnp.where(allowed, scores, -1e30)
        peak = jnp.max(masked, axis=3, keepdims=True)
        weights = jnp.where(allowed, jnp.exp(scores - peak), 0.0)
        total = jnp.sum(weights, axis=3)
        summed = jnp.einsum(
            "qjgk,kjd->qjgd", weights.astype(BF16), values, preferred_element_type=F32
        )
        done.append((summed / total[..., None]).astype(BF16).reshape(half, heads * width))
    flat = jnp.concatenate(done, axis=0)
    tp_size, ctx_size = lax.axis_size("tp"), lax.axis_size("ctx")
    quarter, columns = rows // tp_size, out_weight.shape[1]
    partial = jnp.dot(
        lax.all_gather(flat, "ctx", axis=0, tiled=True), out_weight, preferred_element_type=F32
    )
    partial = partial.reshape(ctx_size, tp_size, quarter, columns)
    summed = lax.psum_scatter(partial.astype(BF16), "tp", scatter_dimension=1, tiled=True)
    return summed.reshape(1, ctx_size, 1, quarter, columns)


def solution(mesh):
    sizes = dict(mesh.shape)
    on_line = sizes["tp"] == 4 and sizes["ctx"] == 2 and sizes["pipe"] == 4
    return jax.shard_map(
        shards_line if on_line else shards_any,
        mesh=mesh,
        in_specs=(
            P(("pipe", "ctx"), "tp", None),
            P(("pipe", "ctx"), "tp", None),
            P(("pipe", "ctx"), "tp", None),
            P(("pipe", "ctx")),
            P("tp", "ctx"),
        ),
        out_specs=P("pipe", None, "tp", None, "ctx"),
        check_vma=False,
    )
```
